32 devices in a mesh: pair: 8 (over z, core), rows: 4 (over y, x).
Axes of the slice: x: 2, y: 2, z: 4, core: 2. Of those that a mesh axis runs over, the one named last changes fastest.
Arguments:
- matrix: float32 [2048, 8192], P(('rows', 'pair')), may hold values from -6 to 6
- plan: int32 [16], replicated, may hold values from 0 to 15, each once
Outputs:
- rotated: float32 [2048, 8192], P('rows', 'pair')
The draws below stay inside these ranges and needn't reach their ends.
Inputs may be any that keep to these rules, and one draw needn't show every extreme that they name: `plan`: each block number appears once.
All inputs are finite; a program needn't handle non-finite values.
Results may differ from the reference program's by a relative error of at most 0.0003.
Values sent between devices are 32-bit elements; how exact they have to be, the bound alone decides.
No kernel may reach another device: no remote copies, remote signals or barrier semaphores. Data moves between devices by JAX's collectives and lax.ppermute only.
A program may use at most 64 MiB of HBM per device.

```python
import jax
import jax.numpy as jnp
from jax import lax

BLK = 512
STEPS = 2
BLOCKS = 16
COLS = 8192
ROWS = 2048
N_PAIR = 8


def shard_levels(own_key, shape, split, least, high):
    level, own = 1.0, jax.random.fold_in(own_key, 6)
    for dim, blocks in split:
        heights = jnp.exp(jax.random.uniform(jax.random.fold_in(own, dim), (blocks,), jnp.float32, least / len(split), high / len(split)))
        level = level * jnp.repeat(heights, shape[dim] // blocks).reshape([-1 if axis == dim else 1 for axis in range(len(shape))])
    return level


def bell_draw(stream_key, dims, scale, limit, pieces=(), kind=jnp.bfloat16):
    loudness = shard_levels(stream_key, dims, pieces, -0.22, 0.18) if pieces else 1.0
    values = jax.random.normal(stream_key, dims, jnp.float32) * scale * loudness
    return jnp.minimum(jnp.maximum(values, -limit), limit).astype(kind)


def setup_inputs(seed: int = 0) -> dict:
    keys = jax.random.split(jax.random.key(seed), 3)
    matrix = bell_draw(keys[0], (ROWS, COLS), 1.0, 6.0, ((0, 32),), jnp.float32)
    plan = jax.random.permutation(keys[1], BLOCKS).astype(jnp.int32)
    return dict(matrix=matrix, plan=plan)


epsilon = 1e-06
high = lax.Precision.HIGHEST

def normalize(gram):
    width = gram.shape[0]
    diagonal = jnp.diagonal(gram) + epsilon
    inverse = 1.0 / jnp.sqrt(diagonal)
    normed = gram * inverse[:, None] * inverse[None, :]
    spread = 1.5 * jnp.sqrt(jnp.sum(normed * normed)) / jnp.sqrt(jnp.float32(width))
    scaled_gram = normed / spread
    identity = jnp.eye(width, dtype=jnp.float32)
    first_iter = 0.5 * (3.0 * identity - scaled_gram)
    factor = 0.5 * jnp.sqrt(diagonal) / jnp.sqrt(spread)
    return (scaled_gram, first_iter, inverse, factor, identity)

def pair_step(block):
    gram = jnp.dot(block.T, block, precision=high, preferred_element_type=jnp.float32)
    scaled_gram, first_iter, inverse, factor, identity = normalize(gram)
    second_term = jnp.dot(scaled_gram, first_iter, precision=high, preferred_element_type=jnp.float32)
    middle = 3.0 * identity - jnp.dot(first_iter, second_term, precision=high, preferred_element_type=jnp.float32)
    product = jnp.dot(block * inverse[None, :], middle, precision=high, preferred_element_type=jnp.float32)
    return jnp.dot(product, first_iter, precision=high, preferred_element_type=jnp.float32) * factor[None, :]

def reference(matrix, plan):
    blocks = matrix.reshape(ROWS, BLOCKS, BLK)
    slots = jnp.take(blocks, plan, axis=1)
    uppers = jnp.transpose(slots[:, 0::2, :], (1, 0, 2))
    lowers = jnp.transpose(slots[:, 1::2, :], (1, 0, 2))
    for turn_index in range(STEPS):
        joined = jnp.concatenate([uppers, lowers], axis=2)
        moved = lax.map(pair_step, joined)
        uppers = moved[:, :, :BLK]
        lowers = moved[:, :, BLK:]
        new_uppers = jnp.concatenate([uppers[0:1], lowers[0:1], uppers[1:N_PAIR - 1]], axis=0)
        new_lowers = jnp.concatenate([lowers[1:], uppers[N_PAIR - 1:]], axis=0)
        uppers, lowers = (new_uppers, new_lowers)
    stacked = jnp.stack([uppers, lowers], axis=1)
    return jnp.transpose(stacked, (2, 0, 1, 3)).reshape(ROWS, COLS)
```

```python
import functools

import jax
import jax.numpy as jnp
from jax import lax
from jax.experimental import pallas as pl
from jax.experimental.pallas import tpu as pltpu
from jax.sharding import PartitionSpec as P

BLK = 512
TILE = 128
SPAN = 256

epsilon = 1e-06
f32 = jnp.float32
bf16 = jnp.bfloat16
VMEM = pl.BlockSpec(memory_space=pltpu.VMEM)
SMEM = pl.BlockSpec(memory_space=pltpu.SMEM)
ANY = pl.BlockSpec(memory_space=pl.ANY)

CHUNKS = ((0, 0, 512), (1, 0, 256), (1, 256, 256))


def shape(dims, dtype=f32):
    return jax.ShapeDtypeStruct(dims, dtype)


def params(mib):
    return pltpu.CompilerParams(vmem_limit_bytes=mib * 1024 * 1024)


def cost(macs, moved):
    return pl.CostEstimate(flops=2 * int(macs), bytes_accessed=int(moved), transcendentals=0)


def halves(value):
    top = value.astype(bf16)
    return top, (value - top.astype(f32)).astype(bf16)


def dot(left, right):
    return lax.dot_general(left, right, (((1,), (0,)), ((), ())), preferred_element_type=f32)


def dot_t(left, right):
    return lax.dot_general(left, right, (((0,), (0,)), ((), ())), preferred_element_type=f32)


def three(op, left, right):
    (lh, ll), (rh, rl) = left, right
    return op(lh, rl) + op(ll, rh) + op(lh, rh)


def triangle(first, count):
    return [(first + i, first + j) for i in range(count) for j in range(i + 1)]


def chunk_tiles(index):
    base = [0]
    for _, _, width in CHUNKS:
        base.append(base[-1] + width // TILE)
    lo, hi = base[index], base[index + 1]
    return [(i, j) for i in range(lo, hi) for j in range(lo)] + triangle(lo, hi - lo)


def pick_kernel(pairs, plan_ref, matrix, *rest):
    outs, sems = rest[:-1], rest[-1]
    me = lax.axis_index("pair")
    copies = []
    for shift in range(pairs):
        pair = lax.rem(me + shift, pairs)
        flip = jnp.where((lax.rem(pair, 2) == 0) & (pair > 0), 1, 0)
        for c, (which, start, width) in enumerate(CHUNKS):
            block = plan_ref[2 * pair + (flip if which == 0 else 1 - flip)]
            first = pl.multiple_of(block * BLK + start, TILE)
            k = shift * len(CHUNKS) + c
            copies.append(pltpu.make_async_copy(matrix.at[:, pl.ds(first, width)], outs[k], sems.at[k]))
            copies[-1].start()
    for copy in copies:
        copy.wait()


def pick(matrix, plan, pairs):
    rows = matrix.shape[0]
    outs = [shape((rows, w)) for _ in range(pairs) for _, _, w in CHUNKS]
    flat = pl.pallas_call(
        functools.partial(pick_kernel, pairs),
        out_shape=outs,
        in_specs=[SMEM, ANY],
        out_specs=[ANY] * len(outs),
        scratch_shapes=[pltpu.SemaphoreType.DMA((len(outs),))],
        name="pick",
    )(plan, matrix)
    n = len(CHUNKS)
    return [[flat[s * n + c] for s in range(pairs)] for c in range(n)]


def spread_tiles(packed, outs):
    row = lax.axis_index("rows")
    part = TILE // len(outs)
    for d, out in enumerate(outs):
        k = jnp.bitwise_xor(row, d)
        out[...] = packed[:, pl.ds(pl.multiple_of(k * part, part), part), :]


def gram_kernel(pairs, index, *refs):
    n_prev = index
    prev = [(refs[2 * k], refs[2 * k + 1]) for k in range(n_prev)]
    pieces = refs[2 * n_prev : 2 * n_prev + pairs]
    top, low, *rest = refs[2 * n_prev + pairs :]
    outs, packed = rest[:-1], rest[-1]
    me = lax.axis_index("pair")
    rows, width = pieces[0].shape
    for shift in range(pairs):
        start = pl.multiple_of(lax.rem(me + pairs - shift, pairs) * rows, rows)
        hi, lo = halves(pieces[shift][...])
        top[pl.ds(start, rows), :] = hi
        low[pl.ds(start, rows), :] = lo
    at = 0
    tiles = chunk_tiles(index)
    place = {t: k for k, t in enumerate(tiles)}
    base = sum(w for _, _, w in CHUNKS[:index])
    blocks = []
    first = 0
    for k, (_, _, w) in enumerate(CHUNKS[:index]):
        blocks += [(prev[k], j, first + j) for j in range(0, w, SPAN)]
        first += w
    blocks += [((top, low), j, base + j) for j in range(0, width, SPAN)]
    for i in range(0, width, SPAN):
        left = (top[:, i : i + SPAN], low[:, i : i + SPAN])
        for (th, tl), j, where in blocks:
            if where > base + i:
                continue
            right = (th[:, j : j + SPAN], tl[:, j : j + SPAN])
            full = three(dot_t, left, right)
            for a in range(0, SPAN, TILE):
                for b in range(0, SPAN, TILE):
                    key = ((base + i + a) // TILE, (where + b) // TILE)
                    if key in place:
                        packed[place[key]] = full[a : a + TILE, b : b + TILE]
    spread_tiles(packed, outs)


def gram(pieces, prev, index):
    pairs = len(pieces)
    rows, width = pieces[0].shape
    n = len(chunk_tiles(index))
    groups = lax.axis_size("rows")
    flat = [h for both in prev for h in both]
    out = pl.pallas_call(
        functools.partial(gram_kernel, pairs, index),
        out_shape=[shape((rows * pairs, width), bf16)] * 2 + [shape((n, TILE // groups, TILE))] * groups,
        in_specs=[VMEM] * (len(flat) + pairs),
        out_specs=[VMEM] * (2 + groups),
        scratch_shapes=[pltpu.VMEM((n, TILE, TILE), f32)],
        compiler_params=params(32),
        cost_estimate=cost(3 * n * TILE * TILE * rows * pairs, 8 * rows * pairs * width),
        name="gram" + str(index),
    )(*flat, *pieces)
    return (out[0], out[1]), out[2:]


def flip_rows(x, mask):
    return lax.ppermute(x, "rows", [(i, i ^ mask) for i in range(lax.axis_size("rows"))])


def sum_rows(parts):
    others = range(1, len(parts))
    total = parts[0]
    for got in [flip_rows(parts[d], d) for d in others]:
        total = total + got
    return [total] + [flip_rows(total, d) for d in others]


def swap_near(x, pairs):
    return lax.ppermute(x, "pair", [(i, i ^ 1) for i in range(pairs)])


def swap_far(x, pairs):
    ends = [(0, 0), (pairs - 1, pairs - 1)]
    return lax.ppermute(x, "pair", ends + [(i, ((i + 1) ^ 1) - 1) for i in range(1, pairs - 1)])


def newton_kernel(tile_lists, whole_lists, n_columns, last, *refs):
    refs = list(refs)

    def take(n):
        got = refs[:n]
        del refs[:n]
        return got

    groups = [take(lax.axis_size("rows")) for _ in tile_lists]
    wholes = take(len(whole_lists))
    columns = [take(2) for _ in range(n_columns)]
    out_s, out_q = take(2)
    extra = [] if last else take(7)
    g, x_hi, x_lo, w_hi, w_lo = take(5)
    n_hi, n_lo, a_hi, a_lo, b_hi, b_lo = take(6) if last else extra[:6]
    width = g.shape[0]
    count = width // TILE
    row = lax.axis_index("rows")

    for tiles, parts in zip(tile_lists, groups):
        for t, (i, j) in enumerate(tiles):
            across = slice(j * TILE, (j + 1) * TILE)
            for d, part in enumerate(parts):
                start = i * TILE + jnp.bitwise_xor(row, d) * part.shape[1]
                g[pl.ds(pl.multiple_of(start, part.shape[1]), part.shape[1]), across] = part[t]
    for tiles, part in zip(whole_lists, wholes):
        for t, (i, j) in enumerate(tiles):
            g[i * TILE : (i + 1) * TILE, j * TILE : (j + 1) * TILE] = part[t]
    for tiles in tile_lists + whole_lists:
        for i, j in tiles:
            if i != j:
                value = g[i * TILE : (i + 1) * TILE, j * TILE : (j + 1) * TILE]
                g[j * TILE : (j + 1) * TILE, i * TILE : (i + 1) * TILE] = value.T

    at = 0
    for hi, lo in columns:
        w = hi.shape[1]
        x_hi[:, at : at + w] = hi[...]
        x_lo[:, at : at + w] = lo[...]
        at += w

    eye = lax.broadcasted_iota(jnp.int32, (TILE, TILE), 0) == lax.broadcasted_iota(jnp.int32, (TILE, TILE), 1)
    along, down = [], []
    for i in range(count):
        own = jnp.where(eye, g[i * TILE : (i + 1) * TILE, i * TILE : (i + 1) * TILE], 0.0)
        along.append(jnp.sum(own, axis=0, keepdims=True))
        down.append(jnp.sum(own, axis=1, keepdims=True))
    d_row = jnp.concatenate(along, axis=1) + epsilon
    s_row = lax.rsqrt(d_row)
    s_col = [lax.rsqrt(v + epsilon) for v in down]
    square = jnp.zeros((1, width), f32)
    for i in range(count):
        band = slice(i * TILE, (i + 1) * TILE)
        normed = g[band, :] * s_col[i] * s_row
        g[band, :] = normed
        n_hi[band, :], n_lo[band, :] = halves(normed)
        square = square + jnp.sum(normed * normed, axis=0, keepdims=True)
    spread = jnp.full((1, 1), 1.5, f32) * jnp.sqrt(jnp.sum(square, axis=1, keepdims=True) / width)
    inverse = 1.0 / spread
    factor = 0.0625 * jnp.sqrt(d_row) * lax.rsqrt(spread)

    for i in range(0, width, SPAN):
        band = slice(i, i + SPAN)
        product = three(dot, (n_hi[band, :], n_lo[band, :]), (n_hi[...], n_lo[...]))
        scaled = g[band, :] * inverse
        product = product * (inverse * inverse)
        here = lax.broadcasted_iota(jnp.int32, (SPAN, width), 0) + i == lax.broadcasted_iota(jnp.int32, (SPAN, width), 1)
        weight = jnp.concatenate(s_col[i // TILE : (i + SPAN) // TILE], axis=0)
        a_hi[band, :], a_lo[band, :] = halves((product - 3.0 * scaled + jnp.where(here, 4.0, 0.0)) * weight)
        b_hi[band, :], b_lo[band, :] = halves(product - 6.0 * scaled + jnp.where(here, 5.0, 0.0))

    rows = x_hi.shape[0]
    for i in range(0, rows, SPAN):
        band = slice(i, i + SPAN)
        value = three(dot, (x_hi[band, :], x_lo[band, :]), (a_hi[...], a_lo[...]))
        w_hi[band, :], w_lo[band, :] = halves(value)

    if last:
        swapped = lax.axis_index("pair") == 0
        s_at = pl.multiple_of(jnp.where(swapped, BLK, 0), BLK)
        q_at = pl.multiple_of(jnp.where(swapped, 0, BLK), BLK)
        s_half = jnp.where(swapped, s_row[:, BLK:], s_row[:, :BLK]), jnp.where(swapped, s_row[:, :BLK], s_row[:, BLK:])
        f_half = jnp.where(swapped, factor[:, BLK:], factor[:, :BLK]), jnp.where(swapped, factor[:, :BLK], factor[:, BLK:])
    else:
        s_at, q_at = 0, BLK
        s_half = s_row[:, :BLK], s_row[:, BLK:]
        f_half = factor[:, :BLK], factor[:, BLK:]
        extra[6][...] = d_row
    for out, first, s_part, f_part in ((out_s, s_at, s_half[0], f_half[0]), (out_q, q_at, s_half[1], f_half[1])):
        cols = pl.ds(first, BLK)
        for i in range(0, rows, SPAN):
            band = slice(i, i + SPAN)
            value = three(dot, (w_hi[band, :], w_lo[band, :]), (b_hi[:, cols], b_lo[:, cols]))
            plain = (x_hi[band, cols].astype(f32) + x_lo[band, cols].astype(f32)) * (16.0 * s_part)
            out[band, :] = (value + plain) * f_part


def newton(tile_lists, whole_lists, groups, wholes, columns, last):
    rows = columns[0][0].shape[0]
    width = sum(hi.shape[1] for hi, _ in columns)
    flat = [p for parts in groups for p in parts] + list(wholes) + [h for both in columns for h in both]
    square = [shape((width, width), bf16)] * 6
    outs = [shape((rows, BLK))] * 2 + ([] if last else square + [shape((1, width))])
    scratch = [pltpu.VMEM((width, width), f32)] + [pltpu.VMEM((rows, width), bf16)] * 4
    if last:
        scratch += [pltpu.VMEM((width, width), bf16)] * 6
    return pl.pallas_call(
        functools.partial(newton_kernel, tile_lists, whole_lists, len(columns), last),
        out_shape=outs,
        in_specs=[VMEM] * len(flat),
        out_specs=[VMEM] * len(outs),
        scratch_shapes=scratch,
        compiler_params=params(48),
        cost_estimate=cost(3 * (width**3 + 2 * rows * width**2), 16 * width**2),
        name="newton",
    )(*flat)


def next_kernel(n_hi, n_lo, a_hi, a_lo, b_hi, b_lo, d_ref, s_out, q_out, p_hi, p_lo, t_hi, t_lo):
    width = n_hi.shape[0]
    d_row = d_ref[...]
    eye = lax.broadcasted_iota(jnp.int32, (TILE, TILE), 0) == lax.broadcasted_iota(jnp.int32, (TILE, TILE), 1)
    d_col = [
        jnp.sum(jnp.where(eye, d_row[:, i : i + TILE], 0.0), axis=1, keepdims=True) for i in range(0, width, TILE)
    ]
    total = jnp.zeros((1, 1), f32)
    for i in range(0, width, SPAN):
        band = slice(i, i + SPAN)
        here = lax.broadcasted_iota(jnp.int32, (SPAN, width), 0) + i == lax.broadcasted_iota(jnp.int32, (SPAN, width), 1)
        root = jnp.sqrt(jnp.concatenate(d_col[i // TILE : (i + SPAN) // TILE], axis=0))
        value = three(dot, (a_hi[band, :], a_lo[band, :]), (b_hi[...], b_lo[...]))
        value = value * (0.125 * root) + jnp.where(here, 2.0, 0.0)
        p_hi[band, :], p_lo[band, :] = halves(value)
        n = n_hi[band, :].astype(f32) + n_lo[band, :].astype(f32)
        total = total + jnp.sum(jnp.sum(n * n, axis=0, keepdims=True), axis=1, keepdims=True)
    spread = 1.5 * jnp.sqrt(total / width)
    for i in range(0, width, SPAN):
        band = slice(i, i + SPAN)
        value = three(dot, (n_hi[band, :], n_lo[band, :]), (p_hi[...], p_lo[...]))
        t_hi[band, :], t_lo[band, :] = halves(value)
    quarter = 0.25 / spread
    for out, base in ((s_out, 0), (q_out, BLK)):
        tiles = triangle(0, BLK // TILE)
        place = {t: k for k, t in enumerate(tiles)}
        for i in range(0, BLK, SPAN):
            cols = slice(base, base + i + SPAN)
            left = (p_hi[base + i : base + i + SPAN, :], p_lo[base + i : base + i + SPAN, :])
            full = three(dot, left, (t_hi[:, cols], t_lo[:, cols]))
            for a in range(0, SPAN, TILE):
                for j in range(0, i + a + TILE, TILE):
                    at = base + i + a
                    weight = jnp.sqrt(d_col[at // TILE]) * jnp.sqrt(d_row[:, base + j : base + j + TILE]) * quarter
                    out[place[((i + a) // TILE, j // TILE)]] = full[a : a + TILE, j : j + TILE] * weight


def next_grams(n_hi, n_lo, a_hi, a_lo, b_hi, b_lo, d_row):
    width = n_hi.shape[0]
    n = len(triangle(0, BLK // TILE))
    return pl.pallas_call(
        next_kernel,
        out_shape=[shape((n, TILE, TILE))] * 2,
        in_specs=[VMEM] * 7,
        out_specs=[VMEM] * 2,
        scratch_shapes=[pltpu.VMEM((width, width), bf16)] * 4,
        compiler_params=params(48),
        cost_estimate=cost(3 * 2.5 * width**3, 16 * width**2),
        name="next_grams",
    )(n_hi, n_lo, a_hi, a_lo, b_hi, b_lo, d_row)


def cross_kernel(near, far, near_hi, near_lo, far_hi, far_lo, *rest):
    outs, packed = rest[:-1], rest[-1]
    near_hi[...], near_lo[...] = halves(near[...])
    far_hi[...], far_lo[...] = halves(far[...])
    count = BLK // TILE
    for i in range(0, BLK, SPAN):
        left = (far_hi[:, i : i + SPAN], far_lo[:, i : i + SPAN])
        full = three(dot_t, left, (near_hi[...], near_lo[...]))
        for a in range(0, SPAN, TILE):
            for b in range(0, BLK, TILE):
                packed[(i + a) // TILE * count + b // TILE] = full[a : a + TILE, b : b + TILE]
    spread_tiles(packed, outs)


def cross(near, far):
    rows = near.shape[0]
    n = (BLK // TILE) ** 2
    groups = lax.axis_size("rows")
    out = pl.pallas_call(
        cross_kernel,
        out_shape=[shape((rows, BLK), bf16)] * 4 + [shape((n, TILE // groups, TILE))] * groups,
        in_specs=[VMEM] * 2,
        out_specs=[VMEM] * (4 + groups),
        scratch_shapes=[pltpu.VMEM((n, TILE, TILE), f32)],
        compiler_params=params(32),
        cost_estimate=cost(3 * rows * BLK * BLK, 16 * rows * BLK),
        name="cross",
    )(near, far)
    return (out[0], out[1]), (out[2], out[3]), out[4:]


def per_device(matrix, plan):
    pairs = lax.axis_size("pair")
    chunks = pick(matrix, plan, pairs)
    columns, groups = [], []
    arrived = []
    for pieces in chunks:
        moved = [pieces[0]]
        for shift in range(1, pairs):
            moved.append(lax.ppermute(pieces[shift], "pair", [(i, (i + shift) % pairs) for i in range(pairs)]))
        arrived.append(moved)
    for index, pieces in enumerate(arrived):
        both, parts = gram(pieces, columns, index)
        columns.append(both)
        groups.append(sum_rows(parts))
    tiles = [chunk_tiles(k) for k in range(len(CHUNKS))]
    out_s, out_q, *held = newton(tiles, [], groups, [], columns, False)
    far = swap_far(out_s, pairs)
    near = swap_near(out_q, pairs)
    s_gram, q_gram = next_grams(*held)
    far_gram = swap_far(s_gram, pairs)
    near_gram = swap_near(q_gram, pairs)
    near_pair, far_pair, parts = cross(near, far)
    summed = sum_rows(parts)
    count = BLK // TILE
    crossing = [(count + i, j) for i in range(count) for j in range(count)]
    out_s, out_q = newton(
        [crossing],
        [triangle(0, count), triangle(count, count)],
        [summed],
        [near_gram, far_gram],
        [near_pair, far_pair],
        True,
    )
    far = swap_far(out_s, pairs)
    near = swap_near(out_q, pairs)
    even = lax.rem(lax.axis_index("pair"), 2) == 0
    return jnp.concatenate([jnp.where(even, far, near), jnp.where(even, near, far)], axis=1)


def solution(mesh):
    placed = (P(("rows", "pair"), None), P())
    return jax.shard_map(
        per_device, mesh=mesh, in_specs=placed, out_specs=P("rows", "pair"), check_vma=False
    )
```

```python
import functools

import jax
import jax.numpy as jnp
from jax import lax
from jax.experimental import pallas as pl
from jax.experimental.pallas import tpu as pltpu
from jax.sharding import PartitionSpec as P

BLK = 512
TILE = 128
SPAN = 256

epsilon = 1e-06
f32 = jnp.float32
bf16 = jnp.bfloat16
VMEM = pl.BlockSpec(memory_space=pltpu.VMEM)
SMEM = pl.BlockSpec(memory_space=pltpu.SMEM)
ANY = pl.BlockSpec(memory_space=pl.ANY)

CHUNKS = ((0, 0, 512), (1, 0, 256), (1, 256, 256))


def shape(dims, dtype=f32):
    return jax.ShapeDtypeStruct(dims, dtype)


def params(mib):
    return pltpu.CompilerParams(vmem_limit_bytes=mib * 1024 * 1024)


def cost(macs, moved):
    return pl.CostEstimate(flops=2 * int(macs), bytes_accessed=int(moved), transcendentals=0)


def halves(value):
    top = value.astype(bf16)
    return top, (value - top.astype(f32)).astype(bf16)


def dot(left, right):
    return lax.dot_general(left, right, (((1,), (0,)), ((), ())), preferred_element_type=f32)


def dot_t(left, right):
    return lax.dot_general(left, right, (((0,), (0,)), ((), ())), preferred_element_type=f32)


def three(op, left, right):
    (lh, ll), (rh, rl) = left, right
    return op(lh, rl) + op(ll, rh) + op(lh, rh)


def triangle(first, count):
    return [(first + i, first + j) for i in range(count) for j in range(i + 1)]


def chunk_tiles(index):
    base = [0]
    for _, _, width in CHUNKS:
        base.append(base[-1] + width // TILE)
    lo, hi = base[index], base[index + 1]
    return [(i, j) for i in range(lo, hi) for j in range(lo)] + triangle(lo, hi - lo)


def pick_kernel(plan_ref, matrix, near, own_q, *own_s):
    me = lax.axis_index("pair")
    hops = len(own_s)
    for k in range(hops):
        for other in (0, 1):
            pair = jnp.bitwise_xor(lax.rem(me + 2 * k, 2 * hops), other)
            flip = jnp.where((lax.rem(pair, 2) == 0) & (pair > 0), 1, 0)
            for which in (0, 1):
                block = plan_ref[2 * pair + (flip if which == 0 else 1 - flip)]
                value = matrix[:, pl.ds(pl.multiple_of(block * BLK, BLK), BLK)]
                if other:
                    near[which, k] = value
                elif which:
                    own_q[k] = value
                else:
                    own_s[k][...] = value


def pick(matrix, plan, pairs):
    rows = matrix.shape[0]
    hops = pairs // 2
    outs = [shape((2, hops, rows, BLK)), shape((hops, rows, BLK))] + [shape((rows, BLK))] * hops
    near, own_q, *own_s = pl.pallas_call(
        pick_kernel,
        out_shape=outs,
        in_specs=[SMEM, VMEM],
        out_specs=[VMEM] * len(outs),
        compiler_params=params(16),
        name="pick",
    )(plan, matrix)
    return near, own_q, own_s


def merge_kernel(near, own_q, *outs):
    core = lax.rem(lax.axis_index("pair"), 2)
    hops, rows, _ = own_q.shape
    forward, queues = outs[:hops], outs[hops:]
    mine = pl.multiple_of(core * rows, rows)
    theirs = pl.multiple_of((1 - core) * rows, rows)
    for k in range(hops):
        forward[k][...] = near[0, k]
        for c, (_, start, width) in enumerate(CHUNKS[1:]):
            out = queues[c * hops + k]
            out[pl.ds(mine, rows), :] = own_q[k, :, start : start + width]
            out[pl.ds(theirs, rows), :] = near[1, k, :, start : start + width]


def merge(near, own_q):
    hops, rows, _ = own_q.shape
    outs = [shape((rows, BLK))] * hops
    outs += [shape((2 * rows, w)) for _, _, w in CHUNKS[1:] for _ in range(hops)]
    flat = pl.pallas_call(
        merge_kernel,
        out_shape=outs,
        in_specs=[VMEM] * 2,
        out_specs=[VMEM] * len(outs),
        compiler_params=params(16),
        name="merge",
    )(near, own_q)
    return [flat[i : i + hops] for i in range(0, len(flat), hops)]


def paths(groups):
    row = lax.axis_index("rows")
    if groups != 4:
        return [jnp.bitwise_xor(row, d) for d in range(groups)]
    x, y = lax.rem(row, 2), lax.div(row, 2)
    flip = jnp.bitwise_xor
    return [4 * h + 2 * flip(first, da) + flip(second, db)
            for h, (first, second) in enumerate(((x, y), (y, x))) for da in (0, 1) for db in (0, 1)]


def part_shapes(n, groups):
    if groups != 4:
        return [shape((n, TILE // groups, TILE))] * groups
    one, two = shape((n, TILE // 8, TILE)), shape((2, n, TILE // 8, TILE))
    return [one, one, two] * 2


def spread_tiles(packed, outs, groups):
    places = paths(groups)
    size = TILE // len(places)
    for d, k in enumerate(places):
        value = packed[:, pl.ds(pl.multiple_of(k * size, size), size), :]
        if groups != 4:
            outs[d][...] = value
        elif d % 4 < 2:
            outs[3 * (d // 4) + d % 4][...] = value
        else:
            outs[3 * (d // 4) + 2][d % 4 - 2] = value


def gram_kernel(pairs, index, groups, *refs):
    refs = list(refs)
    prev = [(refs[2 * k], refs[2 * k + 1]) for k in range(index)]
    n_parts = len(part_shapes(1, groups))
    packed = refs.pop()
    outs, refs = refs[-n_parts:], refs[2 * index : -n_parts]
    top, low = refs[-2:]
    pieces = refs[:-2]
    me = lax.axis_index("pair")
    hops = pairs // 2
    rows = top.shape[0] // pairs
    width = top.shape[1]
    for k in range(hops):
        start = lax.rem(me // 2 + hops - k, hops) * (2 * rows)
        if len(pieces) == hops:
            parts = [(pieces[k], start, 2 * rows)]
        else:
            core = lax.rem(me, 2)
            parts = [(pieces[k], start + core * rows, rows), (pieces[hops + k], start + (1 - core) * rows, rows)]
        for piece, at, size in parts:
            here = pl.ds(pl.multiple_of(at, rows), size)
            top[here, :], low[here, :] = halves(piece[...])
    tiles = chunk_tiles(index)
    place = {t: k for k, t in enumerate(tiles)}
    base = sum(w for _, _, w in CHUNKS[:index])
    blocks = []
    first = 0
    for k, (_, _, w) in enumerate(CHUNKS[:index]):
        blocks += [(prev[k], j, first + j) for j in range(0, w, SPAN)]
        first += w
    blocks += [((top, low), j, base + j) for j in range(0, width, SPAN)]
    for i in range(0, width, SPAN):
        left = (top[:, i : i + SPAN], low[:, i : i + SPAN])
        for (th, tl), j, where in blocks:
            if where > base + i:
                continue
            right = (th[:, j : j + SPAN], tl[:, j : j + SPAN])
            full = three(dot_t, left, right)
            for a in range(0, SPAN, TILE):
                for b in range(0, SPAN, TILE):
                    key = ((base + i + a) // TILE, (where + b) // TILE)
                    if key in place:
                        packed[place[key]] = full[a : a + TILE, b : b + TILE]
    spread_tiles(packed, outs, groups)


def gram(pieces, prev, index, pairs):
    width = pieces[0].shape[1]
    rows = pieces[0].shape[0] * len(pieces)
    n = len(chunk_tiles(index))
    groups = lax.axis_size("rows")
    flat = [h for both in prev for h in both]
    outs = [shape((rows, width), bf16)] * 2 + part_shapes(n, groups)
    out = pl.pallas_call(
        functools.partial(gram_kernel, pairs, index, groups),
        out_shape=outs,
        in_specs=[VMEM] * (len(flat) + len(pieces)),
        out_specs=[VMEM] * len(outs),
        scratch_shapes=[pltpu.VMEM((n, TILE, TILE), f32)],
        compiler_params=params(16),
        cost_estimate=cost(3 * n * TILE * TILE * rows, 8 * rows * width),
        name="gram" + str(index),
    )(*flat, *pieces)
    return (out[0], out[1]), out[2:]


def flip_rows(x, mask):
    return lax.ppermute(x, "rows", [(i, i ^ mask) for i in range(lax.axis_size("rows"))])


def sum_rows(parts):
    groups = lax.axis_size("rows")
    if groups != 4:
        others = range(1, groups)
        total = parts[0]
        for got in [flip_rows(parts[d], d) for d in others]:
            total = total + got
        return [total] + [flip_rows(total, d) for d in others]
    got = [flip_rows(parts[2], 1), flip_rows(parts[5], 2)]
    half = [parts[1] + got[0][1], parts[4] + got[1][1]]
    back = [flip_rows(half[0], 2), flip_rows(half[1], 1)]
    done = [parts[0] + got[0][0] + back[0], parts[3] + got[1][0] + back[1]]
    out = []
    for h, (first, second) in enumerate(((1, 2), (2, 1))):
        other = flip_rows(done[h], second)
        out += [done[h], other, flip_rows(done[h], first), flip_rows(other, first)]
    return out


def swap_near(x, pairs):
    return lax.ppermute(x, "pair", [(i, i ^ 1) for i in range(pairs)])


def swap_far(x, pairs):
    ends = [(0, 0), (pairs - 1, pairs - 1)]
    return lax.ppermute(x, "pair", ends + [(i, ((i + 1) ^ 1) - 1) for i in range(1, pairs - 1)])


def newton_kernel(tile_lists, whole_lists, n_columns, last, *refs):
    refs = list(refs)

    def take(n):
        got = refs[:n]
        del refs[:n]
        return got

    places = paths(lax.axis_size("rows"))
    groups = [take(len(places)) for _ in tile_lists]
    wholes = take(len(whole_lists))
    columns = [take(2) for _ in range(n_columns)]
    out_s, plain_q, w_hi, w_lo, b_hi, b_lo, f_ref = take(7)
    extra = [] if last else take(5)
    g, x_hi, x_lo = take(3)
    n_hi, n_lo, a_hi, a_lo = take(4) if last else extra[:4]
    width = g.shape[0]
    count = width // TILE

    for tiles, parts in zip(tile_lists, groups):
        for t, (i, j) in enumerate(tiles):
            across = slice(j * TILE, (j + 1) * TILE)
            for part, place in zip(parts, places):
                start = i * TILE + place * part.shape[1]
                g[pl.ds(pl.multiple_of(start, part.shape[1]), part.shape[1]), across] = part[t]
    for tiles, part in zip(whole_lists, wholes):
        for t, (i, j) in enumerate(tiles):
            g[i * TILE : (i + 1) * TILE, j * TILE : (j + 1) * TILE] = part[t]
    for tiles in tile_lists + whole_lists:
        for i, j in tiles:
            if i != j:
                value = g[i * TILE : (i + 1) * TILE, j * TILE : (j + 1) * TILE]
                g[j * TILE : (j + 1) * TILE, i * TILE : (i + 1) * TILE] = value.T

    at = 0
    for hi, lo in columns:
        w = hi.shape[1]
        x_hi[:, at : at + w] = hi[...]
        x_lo[:, at : at + w] = lo[...]
        at += w

    eye = lax.broadcasted_iota(jnp.int32, (TILE, TILE), 0) == lax.broadcasted_iota(jnp.int32, (TILE, TILE), 1)
    along, down = [], []
    for i in range(count):
        own = jnp.where(eye, g[i * TILE : (i + 1) * TILE, i * TILE : (i + 1) * TILE], 0.0)
        along.append(jnp.sum(own, axis=0, keepdims=True))
        down.append(jnp.sum(own, axis=1, keepdims=True))
    d_row = jnp.concatenate(along, axis=1) + epsilon
    s_row = lax.rsqrt(d_row)
    s_col = [lax.rsqrt(v + epsilon) for v in down]
    square = jnp.zeros((1, width), f32)
    for i in range(count):
        band = slice(i * TILE, (i + 1) * TILE)
        normed = g[band, :] * s_col[i] * s_row
        g[band, :] = normed
        n_hi[band, :], n_lo[band, :] = halves(normed)
        square = square + jnp.sum(normed * normed, axis=0, keepdims=True)
    spread = jnp.full((1, 1), 1.5, f32) * jnp.sqrt(jnp.sum(square, axis=1, keepdims=True) / width)
    inverse = 1.0 / spread
    factor = 0.0625 * jnp.sqrt(d_row) * lax.rsqrt(spread)

    for i in range(0, width, SPAN):
        band = slice(i, i + SPAN)
        product = three(dot, (n_hi[band, :], n_lo[band, :]), (n_hi[...], n_lo[...]))
        scaled = g[band, :] * inverse
        product = product * (inverse * inverse)
        here = lax.broadcasted_iota(jnp.int32, (SPAN, width), 0) + i == lax.broadcasted_iota(jnp.int32, (SPAN, width), 1)
        weight = jnp.concatenate(s_col[i // TILE : (i + SPAN) // TILE], axis=0)
        a_hi[band, :], a_lo[band, :] = halves((product - 3.0 * scaled + jnp.where(here, 4.0, 0.0)) * weight)
        b_hi[band, :], b_lo[band, :] = halves(product - 6.0 * scaled + jnp.where(here, 5.0, 0.0))

    rows = x_hi.shape[0]
    for i in range(0, rows, SPAN):
        band = slice(i, i + SPAN)
        value = three(dot, (x_hi[band, :], x_lo[band, :]), (a_hi[...], a_lo[...]))
        w_hi[band, :], w_lo[band, :] = halves(value)

    f_ref[...] = factor
    if last:
        s_at, q_at = ends()
    else:
        s_at, q_at = 0, BLK
        extra[4][...] = d_row
    for i in range(0, rows, SPAN):
        band = slice(i, i + SPAN)
        cols = pl.ds(s_at, BLK)
        value = three(dot, (w_hi[band, :], w_lo[band, :]), (b_hi[:, cols], b_lo[:, cols]))
        plain = x_hi[band, :].astype(f32) + x_lo[band, :].astype(f32)
        plain = plain * (16.0 * s_row * factor)
        if last:
            swapped = lax.axis_index("pair") == 0
            left, right, f_left, f_right = plain[:, :BLK], plain[:, BLK:], factor[:, :BLK], factor[:, BLK:]
            out_s[band, :] = value * jnp.where(swapped, f_right, f_left) + jnp.where(swapped, right, left)
            plain_q[band, :] = jnp.where(swapped, left, right)
        else:
            out_s[band, :] = value * factor[:, :BLK] + plain[:, :BLK]
            plain_q[band, :] = plain[:, BLK:]


def ends():
    swapped = lax.axis_index("pair") == 0
    return pl.multiple_of(jnp.where(swapped, BLK, 0), BLK), pl.multiple_of(jnp.where(swapped, 0, BLK), BLK)


def rest_kernel(last, plain_q, w_hi, w_lo, b_hi, b_lo, f_ref, out_q):
    cols = pl.ds(ends()[1] if last else BLK, BLK)
    factor = f_ref[...][:, BLK:]
    if last:
        factor = jnp.where(lax.axis_index("pair") == 0, f_ref[...][:, :BLK], factor)
    for i in range(0, plain_q.shape[0], SPAN):
        band = slice(i, i + SPAN)
        value = three(dot, (w_hi[band, :], w_lo[band, :]), (b_hi[:, cols], b_lo[:, cols]))
        out_q[band, :] = value * factor + plain_q[band, :]


def rest(held, last):
    rows, width = held[1].shape
    return pl.pallas_call(
        functools.partial(rest_kernel, last),
        out_shape=shape((rows, BLK)),
        in_specs=[VMEM] * 6,
        out_specs=VMEM,
        compiler_params=params(12),
        cost_estimate=cost(3 * rows * width * BLK, 8 * rows * width),
        name="rest",
    )(*held)


def newton(tile_lists, whole_lists, groups, wholes, columns, last):
    rows = columns[0][0].shape[0]
    width = sum(hi.shape[1] for hi, _ in columns)
    flat = [p for parts in groups for p in parts] + list(wholes) + [h for both in columns for h in both]
    square = [shape((width, width), bf16)] * 4
    tall = [shape((rows, width), bf16)] * 2
    outs = [shape((rows, BLK))] * 2 + tall + square[:2] + [shape((1, width))]
    outs += [] if last else square + [shape((1, width))]
    scratch = [pltpu.VMEM((width, width), f32)] + [pltpu.VMEM((rows, width), bf16)] * 2
    if last:
        scratch += [pltpu.VMEM((width, width), bf16)] * 4
    return pl.pallas_call(
        functools.partial(newton_kernel, tile_lists, whole_lists, len(columns), last),
        out_shape=outs,
        in_specs=[VMEM] * len(flat),
        out_specs=[VMEM] * len(outs),
        scratch_shapes=scratch,
        compiler_params=params(28),
        cost_estimate=cost(3 * (width**3 + 1.5 * rows * width**2), 16 * width**2),
        name="newton",
    )(*flat)


def flip_line(row):
    eye = lax.broadcasted_iota(jnp.int32, (TILE, TILE), 0) == lax.broadcasted_iota(jnp.int32, (TILE, TILE), 1)
    parts = [jnp.where(eye, row[:, i : i + TILE], 0.0) for i in range(0, row.shape[1], TILE)]
    return [jnp.sum(part, axis=1, keepdims=True) for part in parts]


def power_kernel(n_hi, n_lo, a_hi, a_lo, b_hi, b_lo, d_ref, p_hi, p_lo, t_hi, t_lo):
    width = n_hi.shape[0]
    d_col = flip_line(d_ref[...])
    for i in range(0, width, SPAN):
        band = slice(i, i + SPAN)
        here = lax.broadcasted_iota(jnp.int32, (SPAN, width), 0) + i == lax.broadcasted_iota(jnp.int32, (SPAN, width), 1)
        root = jnp.sqrt(jnp.concatenate(d_col[i // TILE : (i + SPAN) // TILE], axis=0))
        value = three(dot, (a_hi[band, :], a_lo[band, :]), (b_hi[...], b_lo[...]))
        p_hi[band, :], p_lo[band, :] = halves(value * (0.125 * root) + jnp.where(here, 2.0, 0.0))
    for i in range(0, width, SPAN):
        band = slice(i, i + SPAN)
        value = three(dot, (n_hi[band, :], n_lo[band, :]), (p_hi[...], p_lo[...]))
        t_hi[band, :], t_lo[band, :] = halves(value)


def powers(n_hi, n_lo, a_hi, a_lo, b_hi, b_lo, d_row):
    width = n_hi.shape[0]
    return pl.pallas_call(
        power_kernel,
        out_shape=[shape((width, width), bf16)] * 4,
        in_specs=[VMEM] * 7,
        out_specs=[VMEM] * 4,
        compiler_params=params(24),
        cost_estimate=cost(3 * 2 * width**3, 16 * width**2),
        name="powers",
    )(n_hi, n_lo, a_hi, a_lo, b_hi, b_lo, d_row)


def next_kernel(p_hi, p_lo, t_hi, t_lo, f_ref, s_out, q_out):
    f_row = f_ref[...] * 8.0
    f_col = flip_line(f_row)
    for out, base in ((s_out, 0), (q_out, BLK)):
        place = {t: k for k, t in enumerate(triangle(0, BLK // TILE))}
        for i in range(base, base + BLK, SPAN):
            cols = slice(base, i + SPAN)
            full = three(dot, (p_hi[i : i + SPAN, :], p_lo[i : i + SPAN, :]), (t_hi[:, cols], t_lo[:, cols]))
            for at in range(i, i + SPAN, TILE):
                for j in range(base, at + TILE, TILE):
                    tile = full[at - i : at - i + TILE, j - base : j - base + TILE]
                    tile = tile * f_col[at // TILE] * f_row[:, j : j + TILE]
                    out[place[((at - base) // TILE, (j - base) // TILE)]] = tile


def next_grams(p_hi, p_lo, t_hi, t_lo, f_row):
    width = p_hi.shape[0]
    n = len(triangle(0, BLK // TILE))
    return pl.pallas_call(
        next_kernel,
        out_shape=[shape((n, TILE, TILE))] * 2,
        in_specs=[VMEM] * 5,
        out_specs=[VMEM] * 2,
        compiler_params=params(16),
        cost_estimate=cost(3 * 0.5 * width**3, 8 * width**2),
        name="next_grams",
    )(p_hi, p_lo, t_hi, t_lo, f_row)


def cross_kernel(groups, near, far, near_hi, near_lo, far_hi, far_lo, *rest):
    outs, packed = rest[:-1], rest[-1]
    near_hi[...], near_lo[...] = halves(near[...])
    far_hi[...], far_lo[...] = halves(far[...])
    count = BLK // TILE
    for i in range(0, BLK, SPAN):
        left = (far_hi[:, i : i + SPAN], far_lo[:, i : i + SPAN])
        full = three(dot_t, left, (near_hi[...], near_lo[...]))
        for a in range(0, SPAN, TILE):
            for b in range(0, BLK, TILE):
                packed[(i + a) // TILE * count + b // TILE] = full[a : a + TILE, b : b + TILE]
    spread_tiles(packed, outs, groups)


def cross(near, far):
    rows = near.shape[0]
    n = (BLK // TILE) ** 2
    groups = lax.axis_size("rows")
    outs = [shape((rows, BLK), bf16)] * 4 + part_shapes(n, groups)
    out = pl.pallas_call(
        functools.partial(cross_kernel, groups),
        out_shape=outs,
        in_specs=[VMEM] * 2,
        out_specs=[VMEM] * len(outs),
        scratch_shapes=[pltpu.VMEM((n, TILE, TILE), f32)],
        compiler_params=params(16),
        cost_estimate=cost(3 * rows * BLK * BLK, 16 * rows * BLK),
        name="cross",
    )(near, far)
    return (out[0], out[1]), (out[2], out[3]), out[4:]


def around(x, pairs, hop):
    return lax.ppermute(x, "pair", [(i, (i + 2 * hop) % pairs) for i in range(pairs)])


def after(values, first):
    return lax.optimization_barrier((values, first))[0]


def per_device(matrix, plan):
    pairs = lax.axis_size("pair")
    hops = pairs // 2
    near, own_q, own_s = pick(matrix, plan, pairs)
    near = swap_near(near, pairs)
    s_mine = [own_s[0]] + [around(own_s[k], pairs, k) for k in range(1, hops)]
    forward, *queues = merge(near, own_q)
    s_theirs = [forward[0]] + [around(forward[k], pairs, k) for k in range(1, hops)]
    arrived = [s_mine + s_theirs]
    gate = s_mine
    for queue in queues:
        queue = after(queue, gate)
        gate = [queue[0]] + [around(queue[k], pairs, k) for k in range(1, hops)]
        arrived.append(gate)
        gate = s_theirs
    columns, groups = [], []
    for index, pieces in enumerate(arrived):
        both, parts = gram(pieces, columns, index, pairs)
        columns.append(both)
        groups.append(sum_rows(parts))
    tiles = [chunk_tiles(k) for k in range(len(CHUNKS))]
    out_s, *held = newton(tiles, [], groups, [], columns, False)
    held, (n_hi, n_lo, a_hi, a_lo, d_row) = held[:6], held[6:]
    far = swap_far(out_s, pairs)
    near = swap_near(rest(held, False), pairs)
    power = powers(n_hi, n_lo, a_hi, a_lo, held[3], held[4], d_row)
    near, far = after((near, far), power)
    near_pair, far_pair, parts = cross(near, far)
    s_gram, q_gram = next_grams(*after(power, parts), held[5])
    far_gram = swap_far(s_gram, pairs)
    near_gram = swap_near(q_gram, pairs)
    summed = sum_rows(parts)
    count = BLK // TILE
    crossing = [(count + i, j) for i in range(count) for j in range(count)]
    out_s, *held = newton(
        [crossing],
        [triangle(0, count), triangle(count, count)],
        [summed],
        [near_gram, far_gram],
        [near_pair, far_pair],
        True,
    )
    far = swap_far(out_s, pairs)
    near = swap_near(rest(held, True), pairs)
    even = lax.rem(lax.axis_index("pair"), 2) == 0
    return jnp.concatenate([jnp.where(even, far, near), jnp.where(even, near, far)], axis=1)


def solution(mesh):
    placed = (P(("rows", "pair"), None), P())
    return jax.shard_map(
        per_device, mesh=mesh, in_specs=placed, out_specs=P("rows", "pair"), check_vma=False
    )
```

```python
import functools

import jax
import jax.numpy as jnp
from jax import lax
from jax.experimental import pallas as pl
from jax.experimental.pallas import tpu as pltpu
from jax.sharding import PartitionSpec as P

BLK = 512
TILE = 128
SPAN = 256

epsilon = 1e-06
f32 = jnp.float32
bf16 = jnp.bfloat16
VMEM = pl.BlockSpec(memory_space=pltpu.VMEM)
SMEM = pl.BlockSpec(memory_space=pltpu.SMEM)
ANY = pl.BlockSpec(memory_space=pl.ANY)

CHUNKS = ((0, 0, 512), (1, 0, 256), (1, 256, 256))


def shape(dims, dtype=f32):
    return jax.ShapeDtypeStruct(dims, dtype)


def params(mib):
    return pltpu.CompilerParams(vmem_limit_bytes=mib * 1024 * 1024)


def cost(macs, moved):
    return pl.CostEstimate(flops=int(macs) // 64, bytes_accessed=int(moved) // 64, transcendentals=0)


def halves(value):
    top = value.astype(bf16)
    return top, (value - top.astype(f32)).astype(bf16)


def dot(left, right):
    return lax.dot_general(left, right, (((1,), (0,)), ((), ())), preferred_element_type=f32)


def dot_t(left, right):
    return lax.dot_general(left, right, (((0,), (0,)), ((), ())), preferred_element_type=f32)


def three(op, left, right):
    (lh, ll), (rh, rl) = left, right
    return op(lh, rl) + op(ll, rh) + op(lh, rh)


def triangle(first, count):
    return [(first + i, first + j) for i in range(count) for j in range(i + 1)]


ROUNDS = ((0, 1), (2,))


def round_tiles(index):
    return [tile for chunk in ROUNDS[index] for tile in chunk_tiles(chunk)]


def chunk_tiles(index):
    base = [0]
    for _, _, width in CHUNKS:
        base.append(base[-1] + width // TILE)
    lo, hi = base[index], base[index + 1]
    return [(i, j) for i in range(lo, hi) for j in range(lo)] + triangle(lo, hi - lo)


def pick_kernel(plan_ref, matrix, near, own_q, *rest):
    own_s, sems = rest[:-1], rest[-1]
    me = lax.axis_index("pair")
    hops = len(own_s)
    copies = []
    for k in range(hops):
        for other in (1, 0):
            pair = jnp.bitwise_xor(lax.rem(me + 2 * k, 2 * hops), other)
            flip = jnp.where((lax.rem(pair, 2) == 0) & (pair > 0), 1, 0)
            for which in (0, 1):
                block = plan_ref[2 * pair + (flip if which == 0 else 1 - flip)]
                source = matrix.at[:, pl.ds(pl.multiple_of(block * BLK, BLK), BLK)]
                if other:
                    target = near.at[which, k]
                elif which:
                    target = own_q.at[k]
                else:
                    target = own_s[k]
                copies.append(pltpu.make_async_copy(source, target, sems.at[len(copies)]))
                copies[-1].start()
    for copy in copies:
        copy.wait()


def pick(matrix, plan, pairs):
    rows = matrix.shape[0]
    hops = pairs // 2
    outs = [shape((2, hops, rows, BLK)), shape((hops, rows, BLK))] + [shape((rows, BLK))] * hops
    near, own_q, *own_s = pl.pallas_call(
        pick_kernel,
        out_shape=outs,
        in_specs=[SMEM, pl.BlockSpec(memory_space=pltpu.HBM)],
        out_specs=[VMEM] * len(outs),
        scratch_shapes=[pltpu.SemaphoreType.DMA((4 * hops,))],
        compiler_params=params(48),
        name="pick",
    )(plan, matrix)
    return near, own_q, own_s


def merge_kernel(near, own_q, *outs):
    core = lax.rem(lax.axis_index("pair"), 2)
    hops, rows, _ = own_q.shape
    forward, queues = outs[:hops], outs[hops:]
    mine = pl.multiple_of(core * rows, rows)
    theirs = pl.multiple_of((1 - core) * rows, rows)
    for k in range(hops):
        forward[k][...] = near[0, k]
        for c, (_, start, width) in enumerate(CHUNKS[1:]):
            out = queues[c * hops + k]
            out[pl.ds(mine, rows), :] = own_q[k, :, start : start + width]
            out[pl.ds(theirs, rows), :] = near[1, k, :, start : start + width]


def merge(near, own_q):
    hops, rows, _ = own_q.shape
    outs = [shape((rows, BLK))] * hops
    outs += [shape((2 * rows, w)) for _, _, w in CHUNKS[1:] for _ in range(hops)]
    flat = pl.pallas_call(
        merge_kernel,
        out_shape=outs,
        in_specs=[VMEM] * 2,
        out_specs=[VMEM] * len(outs),
        compiler_params=params(16),
        name="merge",
    )(near, own_q)
    return [flat[i : i + hops] for i in range(0, len(flat), hops)]


def paths(groups):
    row = lax.axis_index("rows")
    if groups != 4:
        return [jnp.bitwise_xor(row, d) for d in range(groups)]
    x, y = lax.rem(row, 2), lax.div(row, 2)
    return [x, 1 - x, 2 + y, 3 - y]


def part_shapes(n, groups):
    return [shape((n, TILE // groups, TILE))] * groups


def spread_tiles(packed, outs, groups):
    size = TILE // groups
    for out, k in zip(outs, paths(groups)):
        out[...] = packed[:, pl.ds(pl.multiple_of(k * size, size), size), :]


def gram_kernel(pairs, index, groups, counts, *refs):
    refs = list(refs)
    packed = refs.pop()
    n_prev, n_new = ROUNDS[index][0], len(ROUNDS[index])
    split = [tuple(refs[2 * k : 2 * k + 2]) for k in range(n_prev)]
    del refs[: 2 * n_prev]
    outs = refs[-groups:]
    new = [tuple(refs[2 * k - 2 * n_new - groups :][:2]) for k in range(n_new)]
    me = lax.axis_index("pair")
    core = lax.rem(me, 2)
    hops = pairs // 2
    for (top, low), count in zip(new, counts):
        pieces = refs[:count]
        del refs[:count]
        rows = top.shape[0] // pairs
        for k in range(hops):
            start = lax.rem(me // 2 + hops - k, hops) * (2 * rows)
            if count == hops:
                parts = [(pieces[k], start, 2 * rows)]
            else:
                parts = [(pieces[k], start + core * rows, rows), (pieces[hops + k], start + (1 - core) * rows, rows)]
            for piece, at, size in parts:
                here = pl.ds(pl.multiple_of(at, rows), size)
                top[here, :], low[here, :] = halves(piece[...])
    split += new
    blocks, first = [], 0
    for both in split:
        blocks += [(both, j, first + j) for j in range(0, both[0].shape[1], SPAN)]
        first += both[0].shape[1]
    place = {t: k for k, t in enumerate(round_tiles(index))}
    base = sum(w for _, _, w in CHUNKS[:n_prev])
    for (th, tl), i, row in blocks:
        if row < base:
            continue
        left = (th[:, i : i + SPAN], tl[:, i : i + SPAN])
        for (uh, ul), j, col in blocks:
            if col > row:
                continue
            full = three(dot_t, left, (uh[:, j : j + SPAN], ul[:, j : j + SPAN]))
            for a in range(0, SPAN, TILE):
                for b in range(0, SPAN, TILE):
                    key = ((row + a) // TILE, (col + b) // TILE)
                    if key in place:
                        packed[place[key]] = full[a : a + TILE, b : b + TILE]
    spread_tiles(packed, outs, groups)


def gram(arrays, prev, index, pairs):
    widths = [pieces[0].shape[1] for pieces in arrays]
    rows = arrays[0][0].shape[0] * len(arrays[0])
    n = len(round_tiles(index))
    groups = lax.axis_size("rows")
    flat = [h for both in prev for h in both] + [p for pieces in arrays for p in pieces]
    outs = [shape((rows, w), bf16) for w in widths for _ in (0, 1)] + part_shapes(n, groups)
    out = pl.pallas_call(
        functools.partial(gram_kernel, pairs, index, groups, [len(pieces) for pieces in arrays]),
        out_shape=outs,
        in_specs=[VMEM] * len(flat),
        out_specs=[VMEM] * len(outs),
        scratch_shapes=[pltpu.VMEM((n, TILE, TILE), f32)],
        compiler_params=params(20),
        cost_estimate=cost(10000 * n * TILE * TILE * rows, 8 * rows * sum(widths)),
        name="gram" + str(index),
    )(*flat)
    n_new = len(widths)
    return [(out[2 * k], out[2 * k + 1]) for k in range(n_new)], out[2 * n_new :]


def flip_rows(x, mask):
    return lax.ppermute(x, "rows", [(i, i ^ mask) for i in range(lax.axis_size("rows"))])


def sum_first(parts):
    if len(parts) != 4:
        return [flip_rows(parts[d], d) for d in range(1, len(parts))]
    return [flip_rows(parts[1], 1), flip_rows(parts[3], 2)]


def sum_second(parts, got, gate):
    if len(parts) != 4:
        return [sum(got, parts[0])]
    mine = after([parts[0] + got[0], parts[2] + got[1]], gate)
    return [mine[0] + flip_rows(mine[0], 2), mine[1] + flip_rows(mine[1], 1)]


def sum_spread(done):
    if len(done) == 1:
        return done + [flip_rows(done[0], d) for d in range(1, lax.axis_size("rows"))]
    return [done[0], flip_rows(done[0], 1), done[1], flip_rows(done[1], 2)]


def sum_rows(parts):
    return sum_spread(sum_second(parts, sum_first(parts), []))


def swap_near(x, pairs):
    return lax.ppermute(x, "pair", [(i, i ^ 1) for i in range(pairs)])


def swap_far(x, pairs):
    ends = [(0, 0), (pairs - 1, pairs - 1)]
    return lax.ppermute(x, "pair", ends + [(i, ((i + 1) ^ 1) - 1) for i in range(1, pairs - 1)])


def newton_kernel(tile_lists, whole_lists, n_columns, last, *refs):
    refs = list(refs)

    def take(n):
        got = refs[:n]
        del refs[:n]
        return got

    places = paths(lax.axis_size("rows"))
    groups = [take(len(places)) for _ in tile_lists]
    wholes = take(len(whole_lists))
    columns = [take(2) for _ in range(n_columns)]
    out_s, plain_q, w_hi, w_lo, b_hi, b_lo, f_ref = take(7)
    extra = [] if last else take(5)
    n_hi, n_lo, a_hi, a_lo = take(4) if last else extra[:4]
    tile_ref = refs[0]
    width = n_hi.shape[0]
    count = width // TILE
    row = lax.axis_index("rows")
    x_flip, y_flip = lax.rem(row, 2) == 1, lax.div(row, 2) == 1

    def load(parts, t):
        if len(parts) != 4:
            for part, place in zip(parts, places):
                size = part.shape[1]
                tile_ref[pl.ds(pl.multiple_of(place * size, size), size), :] = part[t]
            return tile_ref[...]
        one, two, three_, four = (part[t] for part in parts)
        rows_ = [jnp.where(x_flip, two, one), jnp.where(x_flip, one, two)]
        rows_ += [jnp.where(y_flip, four, three_), jnp.where(y_flip, three_, four)]
        return jnp.concatenate(rows_, axis=0)

    source = {}
    for tiles, parts in zip(tile_lists, groups):
        for t, key in enumerate(tiles):
            source[key] = functools.partial(load, parts, t)
    for tiles, part in zip(whole_lists, wholes):
        for t, key in enumerate(tiles):
            source[key] = functools.partial(lambda ref, k: ref[k], part, t)

    eye = lax.broadcasted_iota(jnp.int32, (TILE, TILE), 0) == lax.broadcasted_iota(jnp.int32, (TILE, TILE), 1)
    along, down = [], []
    for i in range(count):
        own = jnp.where(eye, source[i, i](), 0.0)
        along.append(jnp.sum(own, axis=0, keepdims=True) + epsilon)
        down.append(jnp.sum(own, axis=1, keepdims=True) + epsilon)
    d_row = jnp.concatenate(along, axis=1)
    s_row = lax.rsqrt(d_row)
    s_col = [lax.rsqrt(v) for v in down]
    square = jnp.zeros((TILE, TILE), f32)
    for (i, j), get in source.items():
        at, to = slice(i * TILE, (i + 1) * TILE), slice(j * TILE, (j + 1) * TILE)
        normed = get() * s_col[i] * s_row[:, to]
        n_hi[at, to], n_lo[at, to] = halves(normed)
        if i == j:
            square = square + normed * normed
        else:
            square = square + 2.0 * (normed * normed)
            n_hi[to, at], n_lo[to, at] = halves(normed.T)
    square = jnp.sum(square, axis=0, keepdims=True)
    spread = jnp.full((1, 1), 1.5, f32) * jnp.sqrt(jnp.sum(square, axis=1, keepdims=True) / width)
    inverse = 1.0 / spread
    factor = 0.0625 * jnp.sqrt(d_row) * lax.rsqrt(spread)

    for i in range(0, width, SPAN):
        band = slice(i, i + SPAN)
        product = three(dot, (n_hi[band, :], n_lo[band, :]), (n_hi[...], n_lo[...]))
        scaled = (n_hi[band, :].astype(f32) + n_lo[band, :].astype(f32)) * inverse
        product = product * (inverse * inverse)
        here = lax.broadcasted_iota(jnp.int32, (SPAN, width), 0) + i == lax.broadcasted_iota(jnp.int32, (SPAN, width), 1)
        weight = jnp.concatenate(s_col[i // TILE : (i + SPAN) // TILE], axis=0)
        a_hi[band, :], a_lo[band, :] = halves((product - 3.0 * scaled + jnp.where(here, 4.0, 0.0)) * weight)
        b_hi[band, :], b_lo[band, :] = halves(product - 6.0 * scaled + jnp.where(here, 5.0, 0.0))

    rows = w_hi.shape[0]

    def wide(k, band):
        return jnp.concatenate([both[k][band, :] for both in columns], axis=1)

    for i in range(0, rows, SPAN):
        band = slice(i, i + SPAN)
        value = three(dot, (wide(0, band), wide(1, band)), (a_hi[...], a_lo[...]))
        w_hi[band, :], w_lo[band, :] = halves(value)

    f_ref[...] = factor
    if last:
        s_at, q_at = ends()
    else:
        s_at, q_at = 0, BLK
        extra[4][...] = d_row
    for i in range(0, rows, SPAN):
        band = slice(i, i + SPAN)
        cols = pl.ds(s_at, BLK)
        value = three(dot, (w_hi[band, :], w_lo[band, :]), (b_hi[:, cols], b_lo[:, cols]))
        plain = wide(0, band).astype(f32) + wide(1, band).astype(f32)
        plain = plain * (16.0 * s_row * factor)
        if last:
            swapped = lax.axis_index("pair") == 0
            left, right, f_left, f_right = plain[:, :BLK], plain[:, BLK:], factor[:, :BLK], factor[:, BLK:]
            out_s[band, :] = value * jnp.where(swapped, f_right, f_left) + jnp.where(swapped, right, left)
            plain_q[band, :] = jnp.where(swapped, left, right)
        else:
            out_s[band, :] = value * factor[:, :BLK] + plain[:, :BLK]
            plain_q[band, :] = plain[:, BLK:]


def ends():
    swapped = lax.axis_index("pair") == 0
    return pl.multiple_of(jnp.where(swapped, BLK, 0), BLK), pl.multiple_of(jnp.where(swapped, 0, BLK), BLK)


def rest_kernel(last, plain_q, w_hi, w_lo, b_hi, b_lo, f_ref, out_q):
    cols = pl.ds(ends()[1] if last else BLK, BLK)
    factor = f_ref[...][:, BLK:]
    if last:
        factor = jnp.where(lax.axis_index("pair") == 0, f_ref[...][:, :BLK], factor)
    for i in range(0, plain_q.shape[0], SPAN):
        band = slice(i, i + SPAN)
        value = three(dot, (w_hi[band, :], w_lo[band, :]), (b_hi[:, cols], b_lo[:, cols]))
        out_q[band, :] = value * factor + plain_q[band, :]


def rest(held, last):
    rows, width = held[1].shape
    return pl.pallas_call(
        functools.partial(rest_kernel, last),
        out_shape=shape((rows, BLK)),
        in_specs=[VMEM] * 6,
        out_specs=VMEM,
        compiler_params=params(12),
        cost_estimate=cost(3000 * rows * width * BLK, 8 * rows * width),
        name="rest",
    )(*held)


def newton(tile_lists, whole_lists, groups, wholes, columns, last):
    rows = columns[0][0].shape[0]
    width = sum(hi.shape[1] for hi, _ in columns)
    flat = [p for parts in groups for p in parts] + list(wholes) + [h for both in columns for h in both]
    square = [shape((width, width), bf16)] * 4
    tall = [shape((rows, width), bf16)] * 2
    outs = [shape((rows, BLK))] * 2 + tall + square[:2] + [shape((1, width))]
    outs += [] if last else square + [shape((1, width))]
    scratch = [pltpu.VMEM((width, width), bf16)] * 4 if last else []
    scratch += [pltpu.VMEM((TILE, TILE), f32)]
    return pl.pallas_call(
        functools.partial(newton_kernel, tile_lists, whole_lists, len(columns), last),
        out_shape=outs,
        in_specs=[VMEM] * len(flat),
        out_specs=[VMEM] * len(outs),
        scratch_shapes=scratch,
        compiler_params=params(28),
        cost_estimate=cost(3 * (width**3 + 1.5 * rows * width**2), 16 * width**2),
        name="newton",
    )(*flat)


def flip_line(row):
    eye = lax.broadcasted_iota(jnp.int32, (TILE, TILE), 0) == lax.broadcasted_iota(jnp.int32, (TILE, TILE), 1)
    parts = [jnp.where(eye, row[:, i : i + TILE], 0.0) for i in range(0, row.shape[1], TILE)]
    return [jnp.sum(part, axis=1, keepdims=True) for part in parts]


def power_kernel(n_hi, n_lo, a_hi, a_lo, b_hi, b_lo, d_ref, p_hi, p_lo, t_hi, t_lo):
    width = n_hi.shape[0]
    d_col = flip_line(d_ref[...])
    for i in range(0, width, SPAN):
        band = slice(i, i + SPAN)
        here = lax.broadcasted_iota(jnp.int32, (SPAN, width), 0) + i == lax.broadcasted_iota(jnp.int32, (SPAN, width), 1)
        root = jnp.sqrt(jnp.concatenate(d_col[i // TILE : (i + SPAN) // TILE], axis=0))
        value = three(dot, (a_hi[band, :], a_lo[band, :]), (b_hi[...], b_lo[...]))
        p_hi[band, :], p_lo[band, :] = halves(value * (0.125 * root) + jnp.where(here, 2.0, 0.0))
    for i in range(0, width, SPAN):
        band = slice(i, i + SPAN)
        value = three(dot, (n_hi[band, :], n_lo[band, :]), (p_hi[...], p_lo[...]))
        t_hi[band, :], t_lo[band, :] = halves(value)


def powers(n_hi, n_lo, a_hi, a_lo, b_hi, b_lo, d_row):
    width = n_hi.shape[0]
    return pl.pallas_call(
        power_kernel,
        out_shape=[shape((width, width), bf16)] * 4,
        in_specs=[VMEM] * 7,
        out_specs=[VMEM] * 4,
        compiler_params=params(24),
        cost_estimate=cost(3 * 2 * width**3, 16 * width**2),
        name="powers",
    )(n_hi, n_lo, a_hi, a_lo, b_hi, b_lo, d_row)


def next_kernel(p_hi, p_lo, t_hi, t_lo, f_ref, s_out, q_out):
    f_row = f_ref[...] * 8.0
    f_col = flip_line(f_row)
    for out, base in ((s_out, 0), (q_out, BLK)):
        place = {t: k for k, t in enumerate(triangle(0, BLK // TILE))}
        for i in range(base, base + BLK, SPAN):
            cols = slice(base, i + SPAN)
            full = three(dot, (p_hi[i : i + SPAN, :], p_lo[i : i + SPAN, :]), (t_hi[:, cols], t_lo[:, cols]))
            for at in range(i, i + SPAN, TILE):
                for j in range(base, at + TILE, TILE):
                    tile = full[at - i : at - i + TILE, j - base : j - base + TILE]
                    tile = tile * f_col[at // TILE] * f_row[:, j : j + TILE]
                    out[place[((at - base) // TILE, (j - base) // TILE)]] = tile


def next_grams(p_hi, p_lo, t_hi, t_lo, f_row):
    width = p_hi.shape[0]
    n = len(triangle(0, BLK // TILE))
    return pl.pallas_call(
        next_kernel,
        out_shape=[shape((n, TILE, TILE))] * 2,
        in_specs=[VMEM] * 5,
        out_specs=[VMEM] * 2,
        compiler_params=params(16),
        cost_estimate=cost(3 * 0.5 * width**3, 8 * width**2),
        name="next_grams",
    )(p_hi, p_lo, t_hi, t_lo, f_row)


def cross_kernel(groups, near, far, near_hi, near_lo, far_hi, far_lo, *rest):
    outs, packed = rest[:-1], rest[-1]
    near_hi[...], near_lo[...] = halves(near[...])
    far_hi[...], far_lo[...] = halves(far[...])
    count = BLK // TILE
    for i in range(0, BLK, SPAN):
        left = (far_hi[:, i : i + SPAN], far_lo[:, i : i + SPAN])
        full = three(dot_t, left, (near_hi[...], near_lo[...]))
        for a in range(0, SPAN, TILE):
            for b in range(0, BLK, TILE):
                packed[(i + a) // TILE * count + b // TILE] = full[a : a + TILE, b : b + TILE]
    spread_tiles(packed, outs, groups)


def cross(near, far):
    rows = near.shape[0]
    n = (BLK // TILE) ** 2
    groups = lax.axis_size("rows")
    outs = [shape((rows, BLK), bf16)] * 4 + part_shapes(n, groups)
    out = pl.pallas_call(
        functools.partial(cross_kernel, groups),
        out_shape=outs,
        in_specs=[VMEM] * 2,
        out_specs=[VMEM] * len(outs),
        scratch_shapes=[pltpu.VMEM((n, TILE, TILE), f32)],
        compiler_params=params(16),
        cost_estimate=cost(3 * rows * BLK * BLK, 16 * rows * BLK),
        name="cross",
    )(near, far)
    return (out[0], out[1]), (out[2], out[3]), out[4:]


def around(x, pairs, hop):
    return lax.ppermute(x, "pair", [(i, (i + 2 * hop) % pairs) for i in range(pairs)])


def after(values, first):
    return lax.optimization_barrier((values, first))[0]


def place_kernel(first, block, kept, out, sem):
    core = lax.rem(lax.axis_index("pair"), 2)
    at = core if first else 1 - core
    half = pl.ds(pl.multiple_of((1 - at) * BLK, BLK), BLK)
    copy = pltpu.make_async_copy(block, out.at[:, half], sem)
    copy.start()
    copy.wait()


def place(block, out):
    first = out is None
    rows = block.shape[0]
    call = pl.pallas_call(
        functools.partial(place_kernel, first),
        out_shape=shape((rows, 2 * BLK)),
        in_specs=[VMEM, SMEM if first else ANY],
        out_specs=ANY,
        scratch_shapes=[pltpu.SemaphoreType.DMA],
        input_output_aliases={} if first else {1: 0},
        compiler_params=params(16),
        name="place",
    )
    return call(block, jnp.zeros((1,), f32) if first else out)


def per_device(matrix, plan):
    pairs = lax.axis_size("pair")
    hops = pairs // 2
    near, own_q, own_s = pick(matrix, plan, pairs)
    near = swap_near(near, pairs)
    s_mine = [own_s[0]] + [around(own_s[k], pairs, k) for k in range(1, hops)]
    forward, *queues = merge(near, own_q)
    s_theirs = [forward[0]] + [around(forward[k], pairs, k) for k in range(1, hops)]
    arrived = [s_mine + s_theirs]
    gate = [s_mine, s_theirs[1]]
    columns, groups = [], []
    done, spread = [], []
    for index, chunks in enumerate(ROUNDS):
        for chunk in chunks:
            if chunk:
                queue = after(queues[chunk - 1], gate)
                arrived.append([queue[0]] + [around(queue[k], pairs, k) for k in range(1, hops)])
        both, parts = gram([arrived[chunk] for chunk in chunks], columns, index, pairs)
        columns += both
        gate = parts
        got = sum_first(parts)
        done = after(sum_second(parts, got, done), spread)
        spread = sum_spread(done)
        groups.append(spread)
    tiles = [round_tiles(k) for k in range(len(ROUNDS))]
    out_s, *held = newton(tiles, [], groups, [], columns, False)
    held, (n_hi, n_lo, a_hi, a_lo, d_row) = held[:6], held[6:]
    far = swap_far(out_s, pairs)
    near = swap_near(rest(held, False), pairs)
    power = powers(n_hi, n_lo, a_hi, a_lo, held[3], held[4], d_row)
    near, far = after((near, far), power)
    near_pair, far_pair, parts = cross(near, far)
    s_gram, q_gram = next_grams(*after(power, parts), held[5])
    far_gram = swap_far(s_gram, pairs)
    near_gram = swap_near(q_gram, pairs)
    summed = sum_rows(parts)
    count = BLK // TILE
    crossing = [(count + i, j) for i in range(count) for j in range(count)]
    out_s, *held = newton(
        [crossing],
        [triangle(0, count), triangle(count, count)],
        [summed],
        [near_gram, far_gram],
        [near_pair, far_pair],
        True,
    )
    far = swap_far(out_s, pairs)
    near = swap_near(rest(held, True), pairs)
    return place(far, place(near, None))


def solution(mesh):
    placed = (P(("rows", "pair"), None), P())
    return jax.shard_map(
        per_device, mesh=mesh, in_specs=placed, out_specs=P("rows", "pair"), check_vma=False
    )
```

```python
import functools

import jax
import jax.numpy as jnp
from jax import lax
from jax.experimental import pallas as pl
from jax.experimental.pallas import tpu as pltpu
from jax.sharding import PartitionSpec as P

BLK = 512
TILE = 128
SPAN = 256

epsilon = 1e-06
f32 = jnp.float32
bf16 = jnp.bfloat16
VMEM = pl.BlockSpec(memory_space=pltpu.VMEM)
SMEM = pl.BlockSpec(memory_space=pltpu.SMEM)
ANY = pl.BlockSpec(memory_space=pl.ANY)

CHUNKS = ((0, 0, 512), (1, 0, 256), (1, 256, 256))


def shape(dims, dtype=f32):
    return jax.ShapeDtypeStruct(dims, dtype)


def params(mib):
    return pltpu.CompilerParams(vmem_limit_bytes=mib * 1024 * 1024)


def cost(macs, moved):
    return pl.CostEstimate(flops=int(macs) // 64, bytes_accessed=int(moved) // 64, transcendentals=0)


def halves(value):
    top = value.astype(bf16)
    return top, (value - top.astype(f32)).astype(bf16)


def dot(left, right):
    return lax.dot_general(left, right, (((1,), (0,)), ((), ())), preferred_element_type=f32)


def dot_t(left, right):
    return lax.dot_general(left, right, (((0,), (0,)), ((), ())), preferred_element_type=f32)


def three(op, left, right):
    (lh, ll), (rh, rl) = left, right
    return op(lh, rl) + op(ll, rh) + op(lh, rh)


def triangle(first, count):
    return [(first + i, first + j) for i in range(count) for j in range(i + 1)]


ROUNDS = ((0, 1), (2,))


def round_tiles(index):
    return [tile for chunk in ROUNDS[index] for tile in chunk_tiles(chunk)]


def chunk_tiles(index):
    base = [0]
    for _, _, width in CHUNKS:
        base.append(base[-1] + width // TILE)
    lo, hi = base[index], base[index + 1]
    return [(i, j) for i in range(lo, hi) for j in range(lo)] + triangle(lo, hi - lo)


def pick_kernel(plan_ref, matrix, near, own_q, *rest):
    own_s, sems = rest[:-1], rest[-1]
    me = lax.axis_index("pair")
    hops = len(own_s)
    copies = []
    for k in range(hops):
        for other in (1, 0):
            pair = jnp.bitwise_xor(lax.rem(me + 2 * k, 2 * hops), other)
            flip = jnp.where((lax.rem(pair, 2) == 0) & (pair > 0), 1, 0)
            for which in (0, 1):
                block = plan_ref[2 * pair + (flip if which == 0 else 1 - flip)]
                source = matrix.at[:, pl.ds(pl.multiple_of(block * BLK, BLK), BLK)]
                if other:
                    target = near.at[which, k]
                elif which:
                    target = own_q.at[k]
                else:
                    target = own_s[k]
                copies.append(pltpu.make_async_copy(source, target, sems.at[len(copies)]))
                copies[-1].start()
    for copy in copies:
        copy.wait()


def pick(matrix, plan, pairs):
    rows = matrix.shape[0]
    hops = pairs // 2
    outs = [shape((2, hops, rows, BLK)), shape((hops, rows, BLK))] + [shape((rows, BLK))] * hops
    near, own_q, *own_s = pl.pallas_call(
        pick_kernel,
        out_shape=outs,
        in_specs=[SMEM, pl.BlockSpec(memory_space=pltpu.HBM)],
        out_specs=[VMEM] * len(outs),
        scratch_shapes=[pltpu.SemaphoreType.DMA((4 * hops,))],
        compiler_params=params(48),
        name="pick",
    )(plan, matrix)
    return near, own_q, own_s


def merge_kernel(near, own_q, *outs):
    core = lax.rem(lax.axis_index("pair"), 2)
    hops, rows, _ = own_q.shape
    forward, queues = outs[:hops], outs[hops:]
    mine = pl.multiple_of(core * rows, rows)
    theirs = pl.multiple_of((1 - core) * rows, rows)
    for k in range(hops):
        forward[k][...] = near[0, k]
        for c, (_, start, width) in enumerate(CHUNKS[1:]):
            out = queues[c * hops + k]
            out[pl.ds(mine, rows), :] = own_q[k, :, start : start + width]
            out[pl.ds(theirs, rows), :] = near[1, k, :, start : start + width]


def merge(near, own_q):
    hops, rows, _ = own_q.shape
    outs = [shape((rows, BLK))] * hops
    outs += [shape((2 * rows, w)) for _, _, w in CHUNKS[1:] for _ in range(hops)]
    flat = pl.pallas_call(
        merge_kernel,
        out_shape=outs,
        in_specs=[VMEM] * 2,
        out_specs=[VMEM] * len(outs),
        compiler_params=params(16),
        name="merge",
    )(near, own_q)
    return [flat[i : i + hops] for i in range(0, len(flat), hops)]


def paths(groups):
    row = lax.axis_index("rows")
    if groups != 4:
        return [jnp.bitwise_xor(row, d) for d in range(groups)]
    x, y = lax.rem(row, 2), lax.div(row, 2)
    return [x, 1 - x, 2 + y, 3 - y]


def part_shapes(n, groups):
    return [shape((n, TILE // groups, TILE))] * groups


def spread_tiles(packed, outs, groups):
    size = TILE // groups
    for out, k in zip(outs, paths(groups)):
        out[...] = packed[:, pl.ds(pl.multiple_of(k * size, size), size), :]


def gram_kernel(pairs, index, groups, counts, *refs):
    refs = list(refs)
    packed = refs.pop()
    n_prev, n_new = ROUNDS[index][0], len(ROUNDS[index])
    split = [tuple(refs[2 * k : 2 * k + 2]) for k in range(n_prev)]
    del refs[: 2 * n_prev]
    outs = refs[-groups:]
    new = [tuple(refs[2 * k - 2 * n_new - groups :][:2]) for k in range(n_new)]
    me = lax.axis_index("pair")
    core = lax.rem(me, 2)
    hops = pairs // 2
    for (top, low), count in zip(new, counts):
        pieces = refs[:count]
        del refs[:count]
        rows = top.shape[0] // pairs
        for k in range(hops):
            start = lax.rem(me // 2 + hops - k, hops) * (2 * rows)
            if count == hops:
                parts = [(pieces[k], start, 2 * rows)]
            else:
                parts = [(pieces[k], start + core * rows, rows), (pieces[hops + k], start + (1 - core) * rows, rows)]
            for piece, at, size in parts:
                here = pl.ds(pl.multiple_of(at, rows), size)
                top[here, :], low[here, :] = halves(piece[...])
    split += new
    blocks, first = [], 0
    for both in split:
        blocks += [(both, j, first + j) for j in range(0, both[0].shape[1], SPAN)]
        first += both[0].shape[1]
    place = {t: k for k, t in enumerate(round_tiles(index))}
    base = sum(w for _, _, w in CHUNKS[:n_prev])
    for (th, tl), i, row in blocks:
        if row < base:
            continue
        left = (th[:, i : i + SPAN], tl[:, i : i + SPAN])
        for (uh, ul), j, col in blocks:
            if col > row:
                continue
            full = three(dot_t, left, (uh[:, j : j + SPAN], ul[:, j : j + SPAN]))
            for a in range(0, SPAN, TILE):
                for b in range(0, SPAN, TILE):
                    key = ((row + a) // TILE, (col + b) // TILE)
                    if key in place:
                        packed[place[key]] = full[a : a + TILE, b : b + TILE]
    spread_tiles(packed, outs, groups)


def gram(arrays, prev, index, pairs):
    widths = [pieces[0].shape[1] for pieces in arrays]
    rows = arrays[0][0].shape[0] * len(arrays[0])
    n = len(round_tiles(index))
    groups = lax.axis_size("rows")
    flat = [h for both in prev for h in both] + [p for pieces in arrays for p in pieces]
    outs = [shape((rows, w), bf16) for w in widths for _ in (0, 1)] + part_shapes(n, groups)
    out = pl.pallas_call(
        functools.partial(gram_kernel, pairs, index, groups, [len(pieces) for pieces in arrays]),
        out_shape=outs,
        in_specs=[VMEM] * len(flat),
        out_specs=[VMEM] * len(outs),
        scratch_shapes=[pltpu.VMEM((n, TILE, TILE), f32)],
        compiler_params=params(20),
        cost_estimate=cost(10000 * n * TILE * TILE * rows, 8 * rows * sum(widths)),
        name="gram" + str(index),
    )(*flat)
    n_new = len(widths)
    return [(out[2 * k], out[2 * k + 1]) for k in range(n_new)], out[2 * n_new :]


def flip_rows(x, mask):
    return lax.ppermute(x, "rows", [(i, i ^ mask) for i in range(lax.axis_size("rows"))])


def sum_first(parts):
    if len(parts) != 4:
        return [flip_rows(parts[d], d) for d in range(1, len(parts))]
    return [flip_rows(parts[1], 1), flip_rows(parts[3], 2)]


def sum_second(parts, got, gate):
    if len(parts) != 4:
        return [sum(got, parts[0])]
    mine = after([parts[0] + got[0], parts[2] + got[1]], gate)
    return [mine[0] + flip_rows(mine[0], 2), mine[1] + flip_rows(mine[1], 1)]


def sum_spread(done):
    if len(done) == 1:
        return done + [flip_rows(done[0], d) for d in range(1, lax.axis_size("rows"))]
    return [done[0], flip_rows(done[0], 1), done[1], flip_rows(done[1], 2)]


def sum_rows(parts):
    return sum_spread(sum_second(parts, sum_first(parts), []))


def swap_near(x, pairs):
    return lax.ppermute(x, "pair", [(i, i ^ 1) for i in range(pairs)])


def swap_far(x, pairs):
    ends = [(0, 0), (pairs - 1, pairs - 1)]
    return lax.ppermute(x, "pair", ends + [(i, ((i + 1) ^ 1) - 1) for i in range(1, pairs - 1)])


def load_tile(parts, t, tile_ref):
    groups = len(parts)
    if groups == 1:
        return parts[0][t]
    if groups != 4:
        for part, place in zip(parts, paths(groups)):
            size = part.shape[1]
            tile_ref[pl.ds(pl.multiple_of(place * size, size), size), :] = part[t]
        return tile_ref[...]
    row = lax.axis_index("rows")
    x_flip, y_flip = lax.rem(row, 2) == 1, lax.div(row, 2) == 1
    a, b, c, d = (part[t] for part in parts)
    pieces = [jnp.where(x_flip, b, a), jnp.where(x_flip, a, b), jnp.where(y_flip, d, c), jnp.where(y_flip, c, d)]
    return jnp.concatenate(pieces, axis=0)


def diagonal_of(value):
    eye = lax.broadcasted_iota(jnp.int32, (TILE, TILE), 0) == lax.broadcasted_iota(jnp.int32, (TILE, TILE), 1)
    return jnp.sum(jnp.where(eye, value, 0.0), axis=0, keepdims=True) + epsilon


def flip_line(row):
    eye = lax.broadcasted_iota(jnp.int32, (TILE, TILE), 0) == lax.broadcasted_iota(jnp.int32, (TILE, TILE), 1)
    parts = [jnp.where(eye, row[:, i : i + TILE], 0.0) for i in range(0, row.shape[1], TILE)]
    return [jnp.sum(part, axis=1, keepdims=True) for part in parts]


def normalize_tiles(tiles, parts, tile_ref, s_row, s_col, n_hi, n_lo):
    square = jnp.zeros((TILE, TILE), f32)
    for t, (i, j) in enumerate(tiles):
        at, to = slice(i * TILE, (i + 1) * TILE), slice(j * TILE, (j + 1) * TILE)
        normed = load_tile(parts, t, tile_ref) * s_col[i] * s_row[:, to]
        n_hi[at, to], n_lo[at, to] = halves(normed)
        if i == j:
            square = square + normed * normed
        else:
            square = square + 2.0 * (normed * normed)
            n_hi[to, at], n_lo[to, at] = halves(normed.T)
    return jnp.sum(square, axis=0, keepdims=True)


def early_kernel(tiles, n_parts, *refs):
    parts, (n_hi, n_lo, own, d_ref, square_ref, tile_ref) = refs[:n_parts], refs[n_parts:]
    width = n_hi.shape[0]
    place = {key: t for t, key in enumerate(tiles)}
    d_row = jnp.concatenate(
        [diagonal_of(load_tile(parts, place[i, i], tile_ref)) for i in range(width // TILE)], axis=1
    )
    d_ref[...] = d_row
    s_row = lax.rsqrt(d_row)
    square_ref[...] = normalize_tiles(tiles, parts, tile_ref, s_row, flip_line(s_row), n_hi, n_lo)
    for i in range(0, width, SPAN):
        band = slice(i, i + SPAN)
        own[band, :] = three(dot, (n_hi[band, :], n_lo[band, :]), (n_hi[...], n_lo[...]))


def early(tiles, parts, width):
    return pl.pallas_call(
        functools.partial(early_kernel, tiles, len(parts)),
        out_shape=[shape((width, width), bf16)] * 2 + [shape((width, width)), shape((1, width)), shape((1, TILE))],
        in_specs=[VMEM] * len(parts),
        out_specs=[VMEM] * 5,
        scratch_shapes=[pltpu.VMEM((TILE, TILE), f32)],
        compiler_params=params(16),
        cost_estimate=cost(100 * width**3, 8 * width**2),
        name="early",
    )(*parts)


def columns_band(columns, band):
    high = jnp.concatenate([hi[band, :] for hi, _ in columns], axis=1)
    low = jnp.concatenate([lo[band, :] for _, lo in columns], axis=1)
    return high, low


def ends(last):
    if not last:
        return 0, BLK
    swapped = lax.axis_index("pair") == 0
    return pl.multiple_of(jnp.where(swapped, BLK, 0), BLK), pl.multiple_of(jnp.where(swapped, 0, BLK), BLK)


def newton_kernel(tiles, n_parts, blocks, n_columns, last, *refs):
    refs = list(refs)

    def take(n):
        got = refs[:n]
        del refs[:n]
        return got

    parts = take(n_parts)
    known = [take(5) for _ in blocks]
    columns = [take(2) for _ in range(n_columns)]
    out_s, out_q = take(2)
    if last:
        tile_ref = take(1)[0]
    n_hi, n_lo, a_hi, a_lo, b_hi, b_lo = take(6)
    if not last:
        d_out, f_out, tile_ref = refs
    width = n_hi.shape[0]
    place = {key: t for t, key in enumerate(tiles)}

    d_parts = [block[3][...] for block in known]
    for i in range(blocks[-1][1] // TILE, width // TILE):
        d_parts.append(diagonal_of(load_tile(parts, place[i, i], tile_ref)))
    d_row = jnp.concatenate(d_parts, axis=1)
    s_row = lax.rsqrt(d_row)
    square = normalize_tiles(tiles, parts, tile_ref, s_row, flip_line(s_row), n_hi, n_lo)
    for (lo, hi), block in zip(blocks, known):
        n_hi[lo:hi, lo:hi] = block[0][...]
        n_lo[lo:hi, lo:hi] = block[1][...]
        square = square + block[4][...]
    spread = jnp.full((1, 1), 1.5, f32) * jnp.sqrt(jnp.sum(square, axis=1, keepdims=True) / width)
    inverse = 1.0 / spread
    factor = 0.0625 * jnp.sqrt(d_row) * lax.rsqrt(spread)
    scale = 16.0 * s_row * factor
    s_col = flip_line(s_row)
    if not last:
        d_out[...] = d_row
        f_out[...] = factor

    for i in range(0, width, SPAN):
        band = slice(i, i + SPAN)
        inside = [k for k, (lo, hi) in enumerate(blocks) if lo <= i < hi]
        if inside:
            lo, hi = blocks[inside[0]]
            rest_ = slice(hi, width) if lo == 0 else slice(0, lo)
            own = three(dot, (n_hi[band, rest_], n_lo[band, rest_]), (n_hi[rest_, lo:hi], n_lo[rest_, lo:hi]))
            own = own + known[inside[0]][2][i - lo : i - lo + SPAN, :]
            other = three(dot, (n_hi[band, :], n_lo[band, :]), (n_hi[:, rest_], n_lo[:, rest_]))
            product = jnp.concatenate([own, other] if lo == 0 else [other, own], axis=1)
        else:
            product = three(dot, (n_hi[band, :], n_lo[band, :]), (n_hi[...], n_lo[...]))
        scaled = (n_hi[band, :].astype(f32) + n_lo[band, :].astype(f32)) * inverse
        product = product * (inverse * inverse)
        here = lax.broadcasted_iota(jnp.int32, (SPAN, width), 0) + i == lax.broadcasted_iota(jnp.int32, (SPAN, width), 1)
        weight = jnp.concatenate(s_col[i // TILE : (i + SPAN) // TILE], axis=0)
        a_hi[band, :], a_lo[band, :] = halves((product - 3.0 * scaled + jnp.where(here, 4.0, 0.0)) * weight)
        b_hi[band, :], b_lo[band, :] = halves(product - 6.0 * scaled + jnp.where(here, 5.0, 0.0))
    swapped = lax.axis_index("pair") == 0
    s_at, q_at = ends(last)
    for i in range(0, out_s.shape[0], SPAN):
        band = slice(i, i + SPAN)
        high, low = columns_band(columns, band)
        w = halves(three(dot, (high, low), (a_hi[...], a_lo[...])))
        plain = (high.astype(f32) + low.astype(f32)) * scale
        near_cols, far_cols = pl.ds(q_at, BLK), pl.ds(s_at, BLK)
        s_value = three(dot, w, (b_hi[:, far_cols], b_lo[:, far_cols]))
        q_value = three(dot, w, (b_hi[:, near_cols], b_lo[:, near_cols]))
        left, right, f_left, f_right = plain[:, :BLK], plain[:, BLK:], factor[:, :BLK], factor[:, BLK:]
        if last:
            left, right = jnp.where(swapped, right, left), jnp.where(swapped, left, right)
            f_left, f_right = jnp.where(swapped, f_right, f_left), jnp.where(swapped, f_left, f_right)
        out_s[band, :] = s_value * f_left + left
        out_q[band, :] = q_value * f_right + right


def newton(tiles, parts, blocks, known, columns, last):
    rows = columns[0][0].shape[0]
    width = sum(hi.shape[1] for hi, _ in columns)
    flat = list(parts) + [v for block in known for v in block] + [h for both in columns for h in both]
    outs = [shape((rows, BLK))] * 2
    scratch = [pltpu.VMEM((TILE, TILE), f32)]
    if last:
        scratch += [pltpu.VMEM((width, width), bf16)] * 6
    else:
        outs += [shape((width, width), bf16)] * 6 + [shape((1, width))] * 2
    return pl.pallas_call(
        functools.partial(newton_kernel, tiles, len(parts), blocks, len(columns), last),
        out_shape=outs,
        in_specs=[VMEM] * len(flat),
        out_specs=[VMEM] * len(outs),
        scratch_shapes=scratch,
        compiler_params=params(28),
        cost_estimate=cost(3 * (width**3 + 2 * rows * width**2), 16 * width**2),
        name="newton",
    )(*flat)


def power_kernel(n_hi, n_lo, a_hi, a_lo, b_hi, b_lo, d_ref, p_hi, p_lo, t_hi, t_lo):
    width = n_hi.shape[0]
    d_col = flip_line(d_ref[...])
    for i in range(0, width, SPAN):
        band = slice(i, i + SPAN)
        here = lax.broadcasted_iota(jnp.int32, (SPAN, width), 0) + i == lax.broadcasted_iota(jnp.int32, (SPAN, width), 1)
        root = jnp.sqrt(jnp.concatenate(d_col[i // TILE : (i + SPAN) // TILE], axis=0))
        value = three(dot, (a_hi[band, :], a_lo[band, :]), (b_hi[...], b_lo[...]))
        p_hi[band, :], p_lo[band, :] = halves(value * (0.125 * root) + jnp.where(here, 2.0, 0.0))
    for i in range(0, width, SPAN):
        band = slice(i, i + SPAN)
        value = three(dot, (n_hi[band, :], n_lo[band, :]), (p_hi[...], p_lo[...]))
        t_hi[band, :], t_lo[band, :] = halves(value)


def powers(n_hi, n_lo, a_hi, a_lo, b_hi, b_lo, d_row):
    width = n_hi.shape[0]
    return pl.pallas_call(
        power_kernel,
        out_shape=[shape((width, width), bf16)] * 4,
        in_specs=[VMEM] * 7,
        out_specs=[VMEM] * 4,
        compiler_params=params(24),
        cost_estimate=cost(3 * 2 * width**3, 16 * width**2),
        name="powers",
    )(n_hi, n_lo, a_hi, a_lo, b_hi, b_lo, d_row)


def next_kernel(p_hi, p_lo, t_hi, t_lo, f_ref, s_out, q_out):
    f_row = f_ref[...] * 8.0
    f_col = flip_line(f_row)
    for out, base in ((s_out, 0), (q_out, BLK)):
        place = {t: k for k, t in enumerate(triangle(0, BLK // TILE))}
        for i in range(base, base + BLK, SPAN):
            cols = slice(base, i + SPAN)
            full = three(dot, (p_hi[i : i + SPAN, :], p_lo[i : i + SPAN, :]), (t_hi[:, cols], t_lo[:, cols]))
            for at in range(i, i + SPAN, TILE):
                for j in range(base, at + TILE, TILE):
                    tile = full[at - i : at - i + TILE, j - base : j - base + TILE]
                    tile = tile * f_col[at // TILE] * f_row[:, j : j + TILE]
                    out[place[((at - base) // TILE, (j - base) // TILE)]] = tile


def next_grams(p_hi, p_lo, t_hi, t_lo, f_row):
    width = p_hi.shape[0]
    n = len(triangle(0, BLK // TILE))
    return pl.pallas_call(
        next_kernel,
        out_shape=[shape((n, TILE, TILE))] * 2,
        in_specs=[VMEM] * 5,
        out_specs=[VMEM] * 2,
        compiler_params=params(16),
        cost_estimate=cost(3 * 0.5 * width**3, 8 * width**2),
        name="next_grams",
    )(p_hi, p_lo, t_hi, t_lo, f_row)


def cross_kernel(groups, near, far, near_hi, near_lo, far_hi, far_lo, *rest):
    outs, packed = rest[:-1], rest[-1]
    near_hi[...], near_lo[...] = halves(near[...])
    far_hi[...], far_lo[...] = halves(far[...])
    count = BLK // TILE
    for i in range(0, BLK, SPAN):
        left = (far_hi[:, i : i + SPAN], far_lo[:, i : i + SPAN])
        full = three(dot_t, left, (near_hi[...], near_lo[...]))
        for a in range(0, SPAN, TILE):
            for b in range(0, BLK, TILE):
                packed[(i + a) // TILE * count + b // TILE] = full[a : a + TILE, b : b + TILE]
    spread_tiles(packed, outs, groups)


def cross(near, far):
    rows = near.shape[0]
    n = (BLK // TILE) ** 2
    groups = lax.axis_size("rows")
    outs = [shape((rows, BLK), bf16)] * 4 + part_shapes(n, groups)
    out = pl.pallas_call(
        functools.partial(cross_kernel, groups),
        out_shape=outs,
        in_specs=[VMEM] * 2,
        out_specs=[VMEM] * len(outs),
        scratch_shapes=[pltpu.VMEM((n, TILE, TILE), f32)],
        compiler_params=params(16),
        cost_estimate=cost(3 * rows * BLK * BLK, 16 * rows * BLK),
        name="cross",
    )(near, far)
    return (out[0], out[1]), (out[2], out[3]), out[4:]


def around(x, pairs, hop):
    return lax.ppermute(x, "pair", [(i, (i + 2 * hop) % pairs) for i in range(pairs)])


def after(values, first):
    return lax.optimization_barrier((values, first))[0]


def place_kernel(near, start, block, kept, out, sem):
    core = lax.rem(lax.axis_index("pair"), 2)
    at = 1 - core if near else core
    cols = pl.ds(pl.multiple_of(at * BLK, BLK), BLK)
    copy = pltpu.make_async_copy(block, out.at[start : start + block.shape[0], cols], sem)
    copy.start()
    copy.wait()


def place(block, start, out, rows):
    first = out is None
    call = pl.pallas_call(
        functools.partial(place_kernel, first, start),
        out_shape=shape((rows, 2 * BLK)),
        in_specs=[VMEM, SMEM if first else ANY],
        out_specs=ANY,
        scratch_shapes=[pltpu.SemaphoreType.DMA],
        input_output_aliases={} if first else {1: 0},
        compiler_params=params(16),
        name="place",
    )
    return call(block, jnp.zeros((1,), f32) if first else out)


def per_device(matrix, plan):
    pairs = lax.axis_size("pair")
    hops = pairs // 2
    near, own_q, own_s = pick(matrix, plan, pairs)
    near = swap_near(near, pairs)
    s_mine = [own_s[0]] + [around(own_s[k], pairs, k) for k in range(1, hops)]
    forward, *queues = merge(near, own_q)
    s_theirs = [forward[0]] + [around(forward[k], pairs, k) for k in range(1, hops)]
    arrived = [s_mine + s_theirs]
    gate = [s_mine, s_theirs[1]]
    columns, groups = [], []
    done, spread = [], []
    for index, chunks in enumerate(ROUNDS):
        for chunk in chunks:
            if chunk:
                queue = after(queues[chunk - 1], gate)
                arrived.append([queue[0]] + [around(queue[k], pairs, k) for k in range(1, hops)])
        both, parts = gram([arrived[chunk] for chunk in chunks], columns, index, pairs)
        columns += both
        gate = parts
        got = sum_first(parts)
        done = after(sum_second(parts, got, done), spread)
        spread = sum_spread(done)
        groups.append(spread)
    edge = sum(CHUNKS[k][2] for k in ROUNDS[0])
    known = early(round_tiles(0), groups[0], edge)
    out_s, out_q, *squares, d_row, f_row = newton(round_tiles(1), groups[1], [(0, edge)], [known], columns, False)
    far, near = swap_far(out_s, pairs), swap_near(out_q, pairs)
    power = powers(*squares, d_row)
    near, far = after((near, far), power)
    near_pair, far_pair, parts = cross(near, far)
    s_gram, q_gram = next_grams(*after(power, parts), f_row)
    far_gram = swap_far(s_gram, pairs)
    near_gram = swap_near(q_gram, pairs)
    summed = sum_rows(parts)
    count = BLK // TILE
    known = [early(triangle(0, count), [tiles], BLK) for tiles in (near_gram, far_gram)]
    crossing = [(count + i, j) for i in range(count) for j in range(count)]
    columns = [near_pair, far_pair]
    out_s, out_q = newton(crossing, summed, [(0, BLK), (BLK, 2 * BLK)], known, columns, True)
    far, near = swap_far(out_s, pairs), swap_near(out_q, pairs)
    return place(far, 0, place(near, 0, None, near.shape[0]), near.shape[0])


def solution(mesh):
    placed = (P(("rows", "pair"), None), P())
    return jax.shard_map(
        per_device, mesh=mesh, in_specs=placed, out_specs=P("rows", "pair"), check_vma=False
    )
```

```python
import functools

import jax
import jax.numpy as jnp
from jax import lax
from jax.experimental import pallas as pl
from jax.experimental.pallas import tpu as pltpu
from jax.sharding import PartitionSpec as P

BLK = 512
TILE = 128
SPAN = 256

epsilon = 1e-06
f32 = jnp.float32
bf16 = jnp.bfloat16
VMEM = pl.BlockSpec(memory_space=pltpu.VMEM)
SMEM = pl.BlockSpec(memory_space=pltpu.SMEM)
ANY = pl.BlockSpec(memory_space=pl.ANY)

CHUNKS = ((0, 0, 512), (1, 0, 256), (1, 256, 256))


def shape(dims, dtype=f32):
    return jax.ShapeDtypeStruct(dims, dtype)


def params(mib):
    return pltpu.CompilerParams(vmem_limit_bytes=mib * 1024 * 1024)


def cost(macs, moved):
    return pl.CostEstimate(flops=int(macs) // 64, bytes_accessed=int(moved) // 64, transcendentals=0)


def halves(value):
    top = value.astype(bf16)
    return top, (value - top.astype(f32)).astype(bf16)


def dot(left, right):
    return lax.dot_general(left, right, (((1,), (0,)), ((), ())), preferred_element_type=f32)


def dot_t(left, right):
    return lax.dot_general(left, right, (((0,), (0,)), ((), ())), preferred_element_type=f32)


def three(op, left, right):
    (lh, ll), (rh, rl) = left, right
    return op(lh, rl) + op(ll, rh) + op(lh, rh)


def triangle(first, count):
    return [(first + i, first + j) for i in range(count) for j in range(i + 1)]


ROUNDS = ((0, 1), (2,))


def round_tiles(index):
    return [tile for chunk in ROUNDS[index] for tile in chunk_tiles(chunk)]


def chunk_tiles(index):
    base = [0]
    for _, _, width in CHUNKS:
        base.append(base[-1] + width // TILE)
    lo, hi = base[index], base[index + 1]
    return [(i, j) for i in range(lo, hi) for j in range(lo)] + triangle(lo, hi - lo)


def pick_kernel(plan_ref, matrix, near, own_q, *rest):
    own_s, sems = rest[:-1], rest[-1]
    me = lax.axis_index("pair")
    hops = len(own_s)
    copies = []
    for k in range(hops):
        for other in (1, 0):
            pair = jnp.bitwise_xor(lax.rem(me + 2 * k, 2 * hops), other)
            flip = jnp.where((lax.rem(pair, 2) == 0) & (pair > 0), 1, 0)
            for which in (0, 1):
                block = plan_ref[2 * pair + (flip if which == 0 else 1 - flip)]
                source = matrix.at[:, pl.ds(pl.multiple_of(block * BLK, BLK), BLK)]
                if other:
                    target = near.at[which, k]
                elif which:
                    target = own_q.at[k]
                else:
                    target = own_s[k]
                copies.append(pltpu.make_async_copy(source, target, sems.at[len(copies)]))
                copies[-1].start()
    for copy in copies:
        copy.wait()


def pick(matrix, plan, pairs):
    rows = matrix.shape[0]
    hops = pairs // 2
    outs = [shape((2, hops, rows, BLK)), shape((hops, rows, BLK))] + [shape((rows, BLK))] * hops
    near, own_q, *own_s = pl.pallas_call(
        pick_kernel,
        out_shape=outs,
        in_specs=[SMEM, pl.BlockSpec(memory_space=pltpu.HBM)],
        out_specs=[VMEM] * len(outs),
        scratch_shapes=[pltpu.SemaphoreType.DMA((4 * hops,))],
        compiler_params=params(48),
        name="pick",
    )(plan, matrix)
    return near, own_q, own_s


def merge_kernel(near, own_q, *outs):
    core = lax.rem(lax.axis_index("pair"), 2)
    hops, rows, _ = own_q.shape
    forward, queues = outs[:hops], outs[hops:]
    mine = pl.multiple_of(core * rows, rows)
    theirs = pl.multiple_of((1 - core) * rows, rows)
    for k in range(hops):
        forward[k][...] = near[0, k]
        for c, (_, start, width) in enumerate(CHUNKS[1:]):
            out = queues[c * hops + k]
            out[pl.ds(mine, rows), :] = own_q[k, :, start : start + width]
            out[pl.ds(theirs, rows), :] = near[1, k, :, start : start + width]


def merge(near, own_q):
    hops, rows, _ = own_q.shape
    outs = [shape((rows, BLK))] * hops
    outs += [shape((2 * rows, w)) for _, _, w in CHUNKS[1:] for _ in range(hops)]
    flat = pl.pallas_call(
        merge_kernel,
        out_shape=outs,
        in_specs=[VMEM] * 2,
        out_specs=[VMEM] * len(outs),
        compiler_params=params(16),
        name="merge",
    )(near, own_q)
    return [flat[i : i + hops] for i in range(0, len(flat), hops)]


def paths(groups):
    row = lax.axis_index("rows")
    if groups != 4:
        return [jnp.bitwise_xor(row, d) for d in range(groups)]
    x, y = lax.rem(row, 2), lax.div(row, 2)
    return [x, 1 - x, 2 + y, 3 - y]


def slots(tiles):
    diagonal = [key for key in tiles if key[0] == key[1]]
    both = [tuple(diagonal[i : i + 2]) for i in range(0, len(diagonal), 2)]
    return [(key,) for key in tiles if key[0] != key[1]] + both


def part_shapes(tiles, groups):
    kept = slots(tiles)
    extra = 8 if any(len(keys) == 2 for keys in kept) else 0
    return [shape((len(kept) * (TILE // groups) + extra, TILE))] * groups


def square_iotas():
    dims = (TILE, TILE)
    return lax.broadcasted_iota(jnp.int32, dims, 0), lax.broadcasted_iota(jnp.int32, dims, 1)


def spread_tiles(packed, extra, outs, groups):
    size = TILE // groups
    count = packed.shape[0] * size
    for out, k in zip(outs, paths(groups)):
        value = packed[:, pl.ds(pl.multiple_of(k * size, size), size), :]
        out[:count, :] = value.reshape(count, TILE)
        if out.shape[0] > count:
            out[count:, :] = extra[...]


def gram_kernel(pairs, index, groups, counts, *refs):
    refs = list(refs)
    extra = refs.pop()
    packed = refs.pop()
    n_prev, n_new = ROUNDS[index][0], len(ROUNDS[index])
    split = [tuple(refs[2 * k : 2 * k + 2]) for k in range(n_prev)]
    del refs[: 2 * n_prev]
    outs = refs[-groups:]
    new = [tuple(refs[2 * k - 2 * n_new - groups :][:2]) for k in range(n_new)]
    me = lax.axis_index("pair")
    core = lax.rem(me, 2)
    hops = pairs // 2
    for (top, low), count in zip(new, counts):
        pieces = refs[:count]
        del refs[:count]
        rows = top.shape[0] // pairs
        for k in range(hops):
            start = lax.rem(me // 2 + hops - k, hops) * (2 * rows)
            if count == hops:
                parts = [(pieces[k], start, 2 * rows)]
            else:
                parts = [(pieces[k], start + core * rows, rows), (pieces[hops + k], start + (1 - core) * rows, rows)]
            for piece, at, size in parts:
                here = pl.ds(pl.multiple_of(at, rows), size)
                top[here, :], low[here, :] = halves(piece[...])
    split += new
    blocks, first = [], 0
    for both in split:
        blocks += [(both, j, first + j) for j in range(0, both[0].shape[1], SPAN)]
        first += both[0].shape[1]
    kept = slots(round_tiles(index))
    singles = sum(len(keys) == 1 for keys in kept)
    place = {key: (k, keys.index(key)) for k, keys in enumerate(kept) for key in keys}
    down, along = square_iotas()
    extra[...] = jnp.zeros_like(extra)
    base = sum(w for _, _, w in CHUNKS[:n_prev])
    for (th, tl), i, row in blocks:
        if row < base:
            continue
        left = (th[:, i : i + SPAN], tl[:, i : i + SPAN])
        for (uh, ul), j, col in blocks:
            if col > row:
                continue
            full = three(dot_t, left, (uh[:, j : j + SPAN], ul[:, j : j + SPAN]))
            for a in range(0, SPAN, TILE):
                for b in range(0, SPAN, TILE):
                    key = ((row + a) // TILE, (col + b) // TILE)
                    if key not in place:
                        continue
                    slot, turn = place[key]
                    tile = full[a : a + TILE, b : b + TILE]
                    if turn:
                        own = jnp.sum(jnp.where(down == along, tile, 0.0), axis=0, keepdims=True)
                        extra[slot - singles : slot - singles + 1, :] = own
                        tile = jnp.where(down >= along, packed[slot], tile)
                    packed[slot] = tile
    spread_tiles(packed, extra, outs, groups)


def gram(arrays, prev, index, pairs):
    widths = [pieces[0].shape[1] for pieces in arrays]
    rows = arrays[0][0].shape[0] * len(arrays[0])
    tiles = round_tiles(index)
    n = len(slots(tiles))
    groups = lax.axis_size("rows")
    flat = [h for both in prev for h in both] + [p for pieces in arrays for p in pieces]
    outs = [shape((rows, w), bf16) for w in widths for _ in (0, 1)] + part_shapes(tiles, groups)
    out = pl.pallas_call(
        functools.partial(gram_kernel, pairs, index, groups, [len(pieces) for pieces in arrays]),
        out_shape=outs,
        in_specs=[VMEM] * len(flat),
        out_specs=[VMEM] * len(outs),
        scratch_shapes=[pltpu.VMEM((n, TILE, TILE), f32), pltpu.VMEM((8, TILE), f32)],
        compiler_params=params(20),
        cost_estimate=cost(10000 * n * TILE * TILE * rows, 8 * rows * sum(widths)),
        name="gram" + str(index),
    )(*flat)
    n_new = len(widths)
    return [(out[2 * k], out[2 * k + 1]) for k in range(n_new)], out[2 * n_new :]


def flip_rows(x, mask):
    return lax.ppermute(x, "rows", [(i, i ^ mask) for i in range(lax.axis_size("rows"))])


def sum_first(parts):
    if len(parts) != 4:
        return [flip_rows(parts[d], d) for d in range(1, len(parts))]
    return [flip_rows(parts[1], 1), flip_rows(parts[3], 2)]


def sum_second(parts, got, gate):
    if len(parts) != 4:
        return [sum(got, parts[0])]
    mine = after([parts[0] + got[0], parts[2] + got[1]], gate)
    return [mine[0] + flip_rows(mine[0], 2), mine[1] + flip_rows(mine[1], 1)]


def sum_spread(done):
    if len(done) == 1:
        return done + [flip_rows(done[0], d) for d in range(1, lax.axis_size("rows"))]
    return [done[0], flip_rows(done[0], 1), done[1], flip_rows(done[1], 2)]


def sum_rows(parts):
    return sum_spread(sum_second(parts, sum_first(parts), []))


def swap_near(x, pairs):
    return lax.ppermute(x, "pair", [(i, i ^ 1) for i in range(pairs)])


def swap_far(x, pairs):
    ends = [(0, 0), (pairs - 1, pairs - 1)]
    return lax.ppermute(x, "pair", ends + [(i, ((i + 1) ^ 1) - 1) for i in range(1, pairs - 1)])


def load_slot(parts, t, tile_ref):
    size = TILE // len(parts)
    pieces = [part[t * size : (t + 1) * size, :] for part in parts]
    if len(parts) != 4:
        for piece, place in zip(pieces, paths(len(parts))):
            tile_ref[pl.ds(pl.multiple_of(place * size, size), size), :] = piece
        return tile_ref[...]
    row = lax.axis_index("rows")
    x_flip, y_flip = lax.rem(row, 2) == 1, lax.div(row, 2) == 1
    a, b, c, d = pieces
    pieces = [jnp.where(x_flip, b, a), jnp.where(x_flip, a, b), jnp.where(y_flip, d, c), jnp.where(y_flip, c, d)]
    return jnp.concatenate(pieces, axis=0)


def tile_reader(tiles, parts, tile_ref):
    if len(parts) == 1:
        return lambda key: parts[0][tiles.index(key)]
    kept = slots(tiles)
    singles = sum(len(keys) == 1 for keys in kept)
    place = {key: (k, keys.index(key)) for k, keys in enumerate(kept) for key in keys}

    def read(key):
        slot, turn = place[key]
        value = load_slot(parts, slot, tile_ref)
        if len(kept[slot]) == 1:
            return value
        down, along = square_iotas()
        if not turn:
            return jnp.where(down >= along, value, value.T)
        at = len(kept) * (TILE // len(parts)) + slot - singles
        return jnp.where(down == along, parts[0][at : at + 1, :], jnp.where(down < along, value, value.T))

    return read


def diagonal_of(value):
    eye = lax.broadcasted_iota(jnp.int32, (TILE, TILE), 0) == lax.broadcasted_iota(jnp.int32, (TILE, TILE), 1)
    return jnp.sum(jnp.where(eye, value, 0.0), axis=0, keepdims=True) + epsilon


def flip_line(row):
    eye = lax.broadcasted_iota(jnp.int32, (TILE, TILE), 0) == lax.broadcasted_iota(jnp.int32, (TILE, TILE), 1)
    parts = [jnp.where(eye, row[:, i : i + TILE], 0.0) for i in range(0, row.shape[1], TILE)]
    return [jnp.sum(part, axis=1, keepdims=True) for part in parts]


def normalize_tiles(tiles, read, s_row, s_col, n_hi, n_lo):
    square = jnp.zeros((TILE, TILE), f32)
    for i, j in tiles:
        at, to = slice(i * TILE, (i + 1) * TILE), slice(j * TILE, (j + 1) * TILE)
        normed = read((i, j)) * s_col[i] * s_row[:, to]
        n_hi[at, to], n_lo[at, to] = halves(normed)
        if i == j:
            square = square + normed * normed
        else:
            square = square + 2.0 * (normed * normed)
            n_hi[to, at], n_lo[to, at] = halves(normed.T)
    return jnp.sum(square, axis=0, keepdims=True)


def early_kernel(tiles, n_parts, *refs):
    parts, (n_hi, n_lo, own, d_ref, square_ref, tile_ref) = refs[:n_parts], refs[n_parts:]
    width = n_hi.shape[0]
    read = tile_reader(tiles, parts, tile_ref)
    d_row = jnp.concatenate([diagonal_of(read((i, i))) for i in range(width // TILE)], axis=1)
    d_ref[...] = d_row
    s_row = lax.rsqrt(d_row)
    square_ref[...] = normalize_tiles(tiles, read, s_row, flip_line(s_row), n_hi, n_lo)
    for i in range(0, width, SPAN):
        band = slice(i, i + SPAN)
        own[band, :] = three(dot, (n_hi[band, :], n_lo[band, :]), (n_hi[...], n_lo[...]))


def early(tiles, parts, width):
    return pl.pallas_call(
        functools.partial(early_kernel, tiles, len(parts)),
        out_shape=[shape((width, width), bf16)] * 2 + [shape((width, width)), shape((1, width)), shape((1, TILE))],
        in_specs=[VMEM] * len(parts),
        out_specs=[VMEM] * 5,
        scratch_shapes=[pltpu.VMEM((TILE, TILE), f32)],
        compiler_params=params(16),
        cost_estimate=cost(100 * width**3, 8 * width**2),
        name="early",
    )(*parts)


def columns_band(columns, band):
    high = jnp.concatenate([hi[band, :] for hi, _ in columns], axis=1)
    low = jnp.concatenate([lo[band, :] for _, lo in columns], axis=1)
    return high, low


def ends(last):
    if not last:
        return 0, BLK
    swapped = lax.axis_index("pair") == 0
    return pl.multiple_of(jnp.where(swapped, BLK, 0), BLK), pl.multiple_of(jnp.where(swapped, 0, BLK), BLK)


def newton_kernel(tiles, n_parts, blocks, n_columns, last, *refs):
    refs = list(refs)

    def take(n):
        got = refs[:n]
        del refs[:n]
        return got

    parts = take(n_parts)
    known = [take(5) for _ in blocks]
    columns = [take(2) for _ in range(n_columns)]
    out_s, out_q = take(2)
    if last:
        tile_ref = take(1)[0]
    n_hi, n_lo, a_hi, a_lo, b_hi, b_lo = take(6)
    if not last:
        d_out, f_out, tile_ref = refs
    width = n_hi.shape[0]
    read = tile_reader(tiles, parts, tile_ref)

    d_parts = [block[3][...] for block in known]
    for i in range(blocks[-1][1] // TILE, width // TILE):
        d_parts.append(diagonal_of(read((i, i))))
    d_row = jnp.concatenate(d_parts, axis=1)
    s_row = lax.rsqrt(d_row)
    square = normalize_tiles(tiles, read, s_row, flip_line(s_row), n_hi, n_lo)
    for (lo, hi), block in zip(blocks, known):
        n_hi[lo:hi, lo:hi] = block[0][...]
        n_lo[lo:hi, lo:hi] = block[1][...]
        square = square + block[4][...]
    spread = jnp.full((1, 1), 1.5, f32) * jnp.sqrt(jnp.sum(square, axis=1, keepdims=True) / width)
    inverse = 1.0 / spread
    factor = 0.0625 * jnp.sqrt(d_row) * lax.rsqrt(spread)
    scale = 16.0 * s_row * factor
    s_col = flip_line(s_row)
    if not last:
        d_out[...] = d_row
        f_out[...] = factor

    for i in range(0, width, SPAN):
        band = slice(i, i + SPAN)
        inside = [k for k, (lo, hi) in enumerate(blocks) if lo <= i < hi]
        if inside:
            lo, hi = blocks[inside[0]]
            rest_ = slice(hi, width) if lo == 0 else slice(0, lo)
            own = three(dot, (n_hi[band, rest_], n_lo[band, rest_]), (n_hi[rest_, lo:hi], n_lo[rest_, lo:hi]))
            own = own + known[inside[0]][2][i - lo : i - lo + SPAN, :]
            other = three(dot, (n_hi[band, :], n_lo[band, :]), (n_hi[:, rest_], n_lo[:, rest_]))
            product = jnp.concatenate([own, other] if lo == 0 else [other, own], axis=1)
        else:
            product = three(dot, (n_hi[band, :], n_lo[band, :]), (n_hi[...], n_lo[...]))
        scaled = (n_hi[band, :].astype(f32) + n_lo[band, :].astype(f32)) * inverse
        product = product * (inverse * inverse)
        here = lax.broadcasted_iota(jnp.int32, (SPAN, width), 0) + i == lax.broadcasted_iota(jnp.int32, (SPAN, width), 1)
        weight = jnp.concatenate(s_col[i // TILE : (i + SPAN) // TILE], axis=0)
        a_hi[band, :], a_lo[band, :] = halves((product - 3.0 * scaled + jnp.where(here, 4.0, 0.0)) * weight)
        b_hi[band, :], b_lo[band, :] = halves(product - 6.0 * scaled + jnp.where(here, 5.0, 0.0))
    swapped = lax.axis_index("pair") == 0
    s_at, q_at = ends(last)
    for i in range(0, out_s.shape[0], SPAN):
        band = slice(i, i + SPAN)
        high, low = columns_band(columns, band)
        w = halves(three(dot, (high, low), (a_hi[...], a_lo[...])))
        plain = (high.astype(f32) + low.astype(f32)) * scale
        near_cols, far_cols = pl.ds(q_at, BLK), pl.ds(s_at, BLK)
        s_value = three(dot, w, (b_hi[:, far_cols], b_lo[:, far_cols]))
        q_value = three(dot, w, (b_hi[:, near_cols], b_lo[:, near_cols]))
        left, right, f_left, f_right = plain[:, :BLK], plain[:, BLK:], factor[:, :BLK], factor[:, BLK:]
        if last:
            left, right = jnp.where(swapped, right, left), jnp.where(swapped, left, right)
            f_left, f_right = jnp.where(swapped, f_right, f_left), jnp.where(swapped, f_left, f_right)
        out_s[band, :] = s_value * f_left + left
        out_q[band, :] = q_value * f_right + right


def newton(tiles, parts, blocks, known, columns, last):
    rows = columns[0][0].shape[0]
    width = sum(hi.shape[1] for hi, _ in columns)
    flat = list(parts) + [v for block in known for v in block] + [h for both in columns for h in both]
    outs = [shape((rows, BLK))] * 2
    scratch = [pltpu.VMEM((TILE, TILE), f32)]
    if last:
        scratch += [pltpu.VMEM((width, width), bf16)] * 6
    else:
        outs += [shape((width, width), bf16)] * 6 + [shape((1, width))] * 2
    return pl.pallas_call(
        functools.partial(newton_kernel, tiles, len(parts), blocks, len(columns), last),
        out_shape=outs,
        in_specs=[VMEM] * len(flat),
        out_specs=[VMEM] * len(outs),
        scratch_shapes=scratch,
        compiler_params=params(28),
        cost_estimate=cost(3 * (width**3 + 2 * rows * width**2), 16 * width**2),
        name="newton",
    )(*flat)


def power_kernel(n_hi, n_lo, a_hi, a_lo, b_hi, b_lo, d_ref, p_hi, p_lo, t_hi, t_lo):
    width = n_hi.shape[0]
    d_col = flip_line(d_ref[...])
    for i in range(0, width, SPAN):
        band = slice(i, i + SPAN)
        here = lax.broadcasted_iota(jnp.int32, (SPAN, width), 0) + i == lax.broadcasted_iota(jnp.int32, (SPAN, width), 1)
        root = jnp.sqrt(jnp.concatenate(d_col[i // TILE : (i + SPAN) // TILE], axis=0))
        value = three(dot, (a_hi[band, :], a_lo[band, :]), (b_hi[...], b_lo[...]))
        p_hi[band, :], p_lo[band, :] = halves(value * (0.125 * root) + jnp.where(here, 2.0, 0.0))
    for i in range(0, width, SPAN):
        band = slice(i, i + SPAN)
        value = three(dot, (n_hi[band, :], n_lo[band, :]), (p_hi[...], p_lo[...]))
        t_hi[band, :], t_lo[band, :] = halves(value)


def powers(n_hi, n_lo, a_hi, a_lo, b_hi, b_lo, d_row):
    width = n_hi.shape[0]
    return pl.pallas_call(
        power_kernel,
        out_shape=[shape((width, width), bf16)] * 4,
        in_specs=[VMEM] * 7,
        out_specs=[VMEM] * 4,
        compiler_params=params(24),
        cost_estimate=cost(3 * 2 * width**3, 16 * width**2),
        name="powers",
    )(n_hi, n_lo, a_hi, a_lo, b_hi, b_lo, d_row)


def next_kernel(p_hi, p_lo, t_hi, t_lo, f_ref, s_out, q_out):
    f_row = f_ref[...] * 8.0
    f_col = flip_line(f_row)
    for out, base in ((s_out, 0), (q_out, BLK)):
        place = {t: k for k, t in enumerate(triangle(0, BLK // TILE))}
        for i in range(base, base + BLK, SPAN):
            cols = slice(base, i + SPAN)
            full = three(dot, (p_hi[i : i + SPAN, :], p_lo[i : i + SPAN, :]), (t_hi[:, cols], t_lo[:, cols]))
            for at in range(i, i + SPAN, TILE):
                for j in range(base, at + TILE, TILE):
                    tile = full[at - i : at - i + TILE, j - base : j - base + TILE]
                    tile = tile * f_col[at // TILE] * f_row[:, j : j + TILE]
                    out[place[((at - base) // TILE, (j - base) // TILE)]] = tile


def next_grams(p_hi, p_lo, t_hi, t_lo, f_row):
    width = p_hi.shape[0]
    n = len(triangle(0, BLK // TILE))
    return pl.pallas_call(
        next_kernel,
        out_shape=[shape((n, TILE, TILE))] * 2,
        in_specs=[VMEM] * 5,
        out_specs=[VMEM] * 2,
        compiler_params=params(16),
        cost_estimate=cost(3 * 0.5 * width**3, 8 * width**2),
        name="next_grams",
    )(p_hi, p_lo, t_hi, t_lo, f_row)


def cross_kernel(groups, near, far, near_hi, near_lo, far_hi, far_lo, *rest):
    outs, packed = rest[:-1], rest[-1]
    near_hi[...], near_lo[...] = halves(near[...])
    far_hi[...], far_lo[...] = halves(far[...])
    count = BLK // TILE
    for i in range(0, BLK, SPAN):
        left = (far_hi[:, i : i + SPAN], far_lo[:, i : i + SPAN])
        full = three(dot_t, left, (near_hi[...], near_lo[...]))
        for a in range(0, SPAN, TILE):
            for b in range(0, BLK, TILE):
                packed[(i + a) // TILE * count + b // TILE] = full[a : a + TILE, b : b + TILE]
    spread_tiles(packed, None, outs, groups)


def cross_tiles():
    count = BLK // TILE
    return [(count + i, j) for i in range(count) for j in range(count)]


def cross(near, far):
    rows = near.shape[0]
    tiles = cross_tiles()
    n = len(tiles)
    groups = lax.axis_size("rows")
    outs = [shape((rows, BLK), bf16)] * 4 + part_shapes(tiles, groups)
    out = pl.pallas_call(
        functools.partial(cross_kernel, groups),
        out_shape=outs,
        in_specs=[VMEM] * 2,
        out_specs=[VMEM] * len(outs),
        scratch_shapes=[pltpu.VMEM((n, TILE, TILE), f32)],
        compiler_params=params(16),
        cost_estimate=cost(3 * rows * BLK * BLK, 16 * rows * BLK),
        name="cross",
    )(near, far)
    return (out[0], out[1]), (out[2], out[3]), out[4:]


def around(x, pairs, hop):
    return lax.ppermute(x, "pair", [(i, (i + 2 * hop) % pairs) for i in range(pairs)])


def after(values, first):
    return lax.optimization_barrier((values, first))[0]


def place_kernel(near, start, block, kept, out, sem):
    core = lax.rem(lax.axis_index("pair"), 2)
    at = 1 - core if near else core
    cols = pl.ds(pl.multiple_of(at * BLK, BLK), BLK)
    copy = pltpu.make_async_copy(block, out.at[start : start + block.shape[0], cols], sem)
    copy.start()
    copy.wait()


def place(block, start, out, rows):
    first = out is None
    call = pl.pallas_call(
        functools.partial(place_kernel, first, start),
        out_shape=shape((rows, 2 * BLK)),
        in_specs=[VMEM, SMEM if first else ANY],
        out_specs=ANY,
        scratch_shapes=[pltpu.SemaphoreType.DMA],
        input_output_aliases={} if first else {1: 0},
        compiler_params=params(16),
        name="place",
    )
    return call(block, jnp.zeros((1,), f32) if first else out)


def per_device(matrix, plan):
    pairs = lax.axis_size("pair")
    hops = pairs // 2
    near, own_q, own_s = pick(matrix, plan, pairs)
    near = swap_near(near, pairs)
    s_mine = [own_s[0]] + [around(own_s[k], pairs, k) for k in range(1, hops)]
    forward, *queues = merge(near, own_q)
    s_theirs = [forward[0]] + [around(forward[k], pairs, k) for k in range(1, hops)]
    arrived = [s_mine + s_theirs]
    gate = [s_mine, s_theirs[1]]
    columns, groups = [], []
    done, spread = [], []
    for index, chunks in enumerate(ROUNDS):
        for chunk in chunks:
            if chunk:
                queue = after(queues[chunk - 1], gate)
                arrived.append([queue[0]] + [around(queue[k], pairs, k) for k in range(1, hops)])
        both, parts = gram([arrived[chunk] for chunk in chunks], columns, index, pairs)
        columns += both
        gate = parts
        got = sum_first(parts)
        done = after(sum_second(parts, got, done), spread)
        spread = sum_spread(done)
        groups.append(spread)
    edge = sum(CHUNKS[k][2] for k in ROUNDS[0])
    known = early(round_tiles(0), groups[0], edge)
    out_s, out_q, *squares, d_row, f_row = newton(round_tiles(1), groups[1], [(0, edge)], [known], columns, False)
    far, near = swap_far(out_s, pairs), swap_near(out_q, pairs)
    power = powers(*squares, d_row)
    near, far = after((near, far), power)
    near_pair, far_pair, parts = cross(near, far)
    s_gram, q_gram = next_grams(*after(power, parts), f_row)
    far_gram = swap_far(s_gram, pairs)
    near_gram = swap_near(q_gram, pairs)
    summed = sum_rows(parts)
    count = BLK // TILE
    known = [early(triangle(0, count), [tiles], BLK) for tiles in (near_gram, far_gram)]
    crossing = cross_tiles()
    columns = [near_pair, far_pair]
    out_s, out_q = newton(crossing, summed, [(0, BLK), (BLK, 2 * BLK)], known, columns, True)
    far, near = swap_far(out_s, pairs), swap_near(out_q, pairs)
    return place(far, 0, place(near, 0, None, near.shape[0]), near.shape[0])


def solution(mesh):
    placed = (P(("rows", "pair"), None), P())
    return jax.shard_map(
        per_device, mesh=mesh, in_specs=placed, out_specs=P("rows", "pair"), check_vma=False
    )
```

```python
import functools

import jax
import jax.numpy as jnp
from jax import lax
from jax.experimental import pallas as pl
from jax.experimental.pallas import tpu as pltpu
from jax.sharding import PartitionSpec as P

BLK = 512
TILE = 128
SPAN = 256
BAND = 512

epsilon = 1e-06
f32 = jnp.float32
bf16 = jnp.bfloat16
VMEM = pl.BlockSpec(memory_space=pltpu.VMEM)
SMEM = pl.BlockSpec(memory_space=pltpu.SMEM)
ANY = pl.BlockSpec(memory_space=pl.ANY)

CHUNKS = ((0, 0, 512), (1, 0, 256), (1, 256, 256))


def shape(dims, dtype=f32):
    return jax.ShapeDtypeStruct(dims, dtype)


def params(mib):
    return pltpu.CompilerParams(vmem_limit_bytes=mib * 1024 * 1024)


def cost(macs, moved):
    return pl.CostEstimate(flops=int(macs) // 64, bytes_accessed=int(moved) // 64, transcendentals=0)


def halves(value):
    top = value.astype(bf16)
    return top, (value - top.astype(f32)).astype(bf16)


def dot(left, right):
    return lax.dot_general(left, right, (((1,), (0,)), ((), ())), preferred_element_type=f32)


def dot_t(left, right):
    return lax.dot_general(left, right, (((0,), (0,)), ((), ())), preferred_element_type=f32)


def three(op, left, right):
    (lh, ll), (rh, rl) = left, right
    return op(lh, rl) + op(ll, rh) + op(lh, rh)


def triangle(first, count):
    return [(first + i, first + j) for i in range(count) for j in range(i + 1)]


ROUNDS = ((0, 1), (2,))


def round_tiles(index):
    return [tile for chunk in ROUNDS[index] for tile in chunk_tiles(chunk)]


def chunk_tiles(index):
    base = [0]
    for _, _, width in CHUNKS:
        base.append(base[-1] + width // TILE)
    lo, hi = base[index], base[index + 1]
    return [(i, j) for i in range(lo, hi) for j in range(lo)] + triangle(lo, hi - lo)


def pick_kernel(plan_ref, matrix, near, own_q, *rest):
    own_s, sems = rest[:-1], rest[-1]
    me = lax.axis_index("pair")
    hops = len(own_s)
    copies = []
    for k in range(hops):
        for other in (1, 0):
            pair = jnp.bitwise_xor(lax.rem(me + 2 * k, 2 * hops), other)
            flip = jnp.where((lax.rem(pair, 2) == 0) & (pair > 0), 1, 0)
            for which in (0, 1):
                block = plan_ref[2 * pair + (flip if which == 0 else 1 - flip)]
                source = matrix.at[:, pl.ds(pl.multiple_of(block * BLK, BLK), BLK)]
                if other:
                    target = near.at[which, k]
                elif which:
                    target = own_q.at[k]
                else:
                    target = own_s[k]
                copies.append(pltpu.make_async_copy(source, target, sems.at[len(copies)]))
                copies[-1].start()
    for copy in copies:
        copy.wait()


def pick(matrix, plan, pairs):
    rows = matrix.shape[0]
    hops = pairs // 2
    outs = [shape((2, hops, rows, BLK)), shape((hops, rows, BLK))] + [shape((rows, BLK))] * hops
    near, own_q, *own_s = pl.pallas_call(
        pick_kernel,
        out_shape=outs,
        in_specs=[SMEM, pl.BlockSpec(memory_space=pltpu.HBM)],
        out_specs=[VMEM] * len(outs),
        scratch_shapes=[pltpu.SemaphoreType.DMA((4 * hops,))],
        compiler_params=params(48),
        name="pick",
    )(plan, matrix)
    return near, own_q, own_s


def merge_kernel(near, own_q, *outs):
    core = lax.rem(lax.axis_index("pair"), 2)
    hops, rows, _ = own_q.shape
    forward, queues = outs[:hops], outs[hops:]
    mine = pl.multiple_of(core * rows, rows)
    theirs = pl.multiple_of((1 - core) * rows, rows)
    for k in range(hops):
        forward[k][...] = near[0, k]
        for c, (_, start, width) in enumerate(CHUNKS[1:]):
            out = queues[c * hops + k]
            out[pl.ds(mine, rows), :] = own_q[k, :, start : start + width]
            out[pl.ds(theirs, rows), :] = near[1, k, :, start : start + width]


def merge(near, own_q):
    hops, rows, _ = own_q.shape
    outs = [shape((rows, BLK))] * hops
    outs += [shape((2 * rows, w)) for _, _, w in CHUNKS[1:] for _ in range(hops)]
    flat = pl.pallas_call(
        merge_kernel,
        out_shape=outs,
        in_specs=[VMEM] * 2,
        out_specs=[VMEM] * len(outs),
        compiler_params=params(16),
        name="merge",
    )(near, own_q)
    return [flat[i : i + hops] for i in range(0, len(flat), hops)]


def paths(groups):
    row = lax.axis_index("rows")
    if groups != 4:
        return [jnp.bitwise_xor(row, d) for d in range(groups)]
    x, y = lax.rem(row, 2), lax.div(row, 2)
    return [x, 1 - x, 2 + y, 3 - y]


def slots(tiles):
    diagonal = [key for key in tiles if key[0] == key[1]]
    both = [tuple(diagonal[i : i + 2]) for i in range(0, len(diagonal), 2)]
    return [(key,) for key in tiles if key[0] != key[1]] + both


def part_shapes(tiles, groups):
    kept = slots(tiles)
    extra = 8 if any(len(keys) == 2 for keys in kept) else 0
    return [shape((len(kept) * (TILE // groups) + extra, TILE))] * groups


def square_iotas():
    dims = (TILE, TILE)
    return lax.broadcasted_iota(jnp.int32, dims, 0), lax.broadcasted_iota(jnp.int32, dims, 1)


def spread_tiles(packed, extra, outs, groups):
    size = TILE // groups
    count = packed.shape[0] * size
    for out, k in zip(outs, paths(groups)):
        value = packed[:, pl.ds(pl.multiple_of(k * size, size), size), :]
        out[:count, :] = value.reshape(count, TILE)
        if out.shape[0] > count:
            out[count:, :] = extra[...]


def gram_kernel(pairs, index, groups, counts, *refs):
    refs = list(refs)
    extra = refs.pop()
    packed = refs.pop()
    n_prev, n_new = ROUNDS[index][0], len(ROUNDS[index])
    split = [tuple(refs[2 * k : 2 * k + 2]) for k in range(n_prev)]
    del refs[: 2 * n_prev]
    outs = refs[-groups:]
    new = [tuple(refs[2 * k - 2 * n_new - groups :][:2]) for k in range(n_new)]
    me = lax.axis_index("pair")
    core = lax.rem(me, 2)
    hops = pairs // 2
    for (top, low), count in zip(new, counts):
        pieces = refs[:count]
        del refs[:count]
        rows = top.shape[0] // pairs
        for k in range(hops):
            start = lax.rem(me // 2 + hops - k, hops) * (2 * rows)
            if count == hops:
                parts = [(pieces[k], start, 2 * rows)]
            else:
                parts = [(pieces[k], start + core * rows, rows), (pieces[hops + k], start + (1 - core) * rows, rows)]
            for piece, at, size in parts:
                here = pl.ds(pl.multiple_of(at, rows), size)
                top[here, :], low[here, :] = halves(piece[...])
    split += new
    blocks, first = [], 0
    for both in split:
        blocks += [(both, j, first + j) for j in range(0, both[0].shape[1], SPAN)]
        first += both[0].shape[1]
    kept = slots(round_tiles(index))
    singles = sum(len(keys) == 1 for keys in kept)
    place = {key: (k, keys.index(key)) for k, keys in enumerate(kept) for key in keys}
    down, along = square_iotas()
    extra[...] = jnp.zeros_like(extra)
    base = sum(w for _, _, w in CHUNKS[:n_prev])
    for (th, tl), i, row in blocks:
        if row < base:
            continue
        left = (th[:, i : i + SPAN], tl[:, i : i + SPAN])
        for (uh, ul), j, col in blocks:
            if col > row:
                continue
            full = three(dot_t, left, (uh[:, j : j + SPAN], ul[:, j : j + SPAN]))
            for a in range(0, SPAN, TILE):
                for b in range(0, SPAN, TILE):
                    key = ((row + a) // TILE, (col + b) // TILE)
                    if key not in place:
                        continue
                    slot, turn = place[key]
                    tile = full[a : a + TILE, b : b + TILE]
                    if turn:
                        own = jnp.sum(jnp.where(down == along, tile, 0.0), axis=0, keepdims=True)
                        extra[slot - singles : slot - singles + 1, :] = own
                        tile = jnp.where(down >= along, packed[slot], tile)
                    packed[slot] = tile
    spread_tiles(packed, extra, outs, groups)


def gram(arrays, prev, index, pairs):
    widths = [pieces[0].shape[1] for pieces in arrays]
    rows = arrays[0][0].shape[0] * len(arrays[0])
    tiles = round_tiles(index)
    n = len(slots(tiles))
    groups = lax.axis_size("rows")
    flat = [h for both in prev for h in both] + [p for pieces in arrays for p in pieces]
    outs = [shape((rows, w), bf16) for w in widths for _ in (0, 1)] + part_shapes(tiles, groups)
    out = pl.pallas_call(
        functools.partial(gram_kernel, pairs, index, groups, [len(pieces) for pieces in arrays]),
        out_shape=outs,
        in_specs=[VMEM] * len(flat),
        out_specs=[VMEM] * len(outs),
        scratch_shapes=[pltpu.VMEM((n, TILE, TILE), f32), pltpu.VMEM((8, TILE), f32)],
        compiler_params=params(20),
        cost_estimate=cost(10000 * n * TILE * TILE * rows, 8 * rows * sum(widths)),
        name="gram" + str(index),
    )(*flat)
    n_new = len(widths)
    return [(out[2 * k], out[2 * k + 1]) for k in range(n_new)], out[2 * n_new :]


def flip_rows(x, mask):
    return lax.ppermute(x, "rows", [(i, i ^ mask) for i in range(lax.axis_size("rows"))])


def sum_first(parts):
    if len(parts) != 4:
        return [flip_rows(parts[d], d) for d in range(1, len(parts))]
    return [flip_rows(parts[1], 1), flip_rows(parts[3], 2)]


def sum_second(parts, got, gate):
    if len(parts) != 4:
        return [sum(got, parts[0])]
    mine = after([parts[0] + got[0], parts[2] + got[1]], gate)
    return [mine[0] + flip_rows(mine[0], 2), mine[1] + flip_rows(mine[1], 1)]


def sum_spread(done):
    if len(done) == 1:
        return done + [flip_rows(done[0], d) for d in range(1, lax.axis_size("rows"))]
    return [done[0], flip_rows(done[0], 1), done[1], flip_rows(done[1], 2)]


def sum_rows(parts):
    return sum_spread(sum_second(parts, sum_first(parts), []))


def swap_near(x, pairs):
    return lax.ppermute(x, "pair", [(i, i ^ 1) for i in range(pairs)])


def swap_far(x, pairs):
    ends = [(0, 0), (pairs - 1, pairs - 1)]
    return lax.ppermute(x, "pair", ends + [(i, ((i + 1) ^ 1) - 1) for i in range(1, pairs - 1)])


def load_slot(parts, t, tile_ref):
    size = TILE // len(parts)
    pieces = [part[t * size : (t + 1) * size, :] for part in parts]
    if len(parts) != 4:
        for piece, place in zip(pieces, paths(len(parts))):
            tile_ref[pl.ds(pl.multiple_of(place * size, size), size), :] = piece
        return tile_ref[...]
    row = lax.axis_index("rows")
    x_flip, y_flip = lax.rem(row, 2) == 1, lax.div(row, 2) == 1
    a, b, c, d = pieces
    pieces = [jnp.where(x_flip, b, a), jnp.where(x_flip, a, b), jnp.where(y_flip, d, c), jnp.where(y_flip, c, d)]
    return jnp.concatenate(pieces, axis=0)


def tile_reader(tiles, parts, tile_ref):
    if len(parts) == 1:
        return lambda key: parts[0][tiles.index(key)]
    kept = slots(tiles)
    singles = sum(len(keys) == 1 for keys in kept)
    place = {key: (k, keys.index(key)) for k, keys in enumerate(kept) for key in keys}

    def read(key):
        slot, turn = place[key]
        value = load_slot(parts, slot, tile_ref)
        if len(kept[slot]) == 1:
            return value
        down, along = square_iotas()
        if not turn:
            return jnp.where(down >= along, value, value.T)
        at = len(kept) * (TILE // len(parts)) + slot - singles
        return jnp.where(down == along, parts[0][at : at + 1, :], jnp.where(down < along, value, value.T))

    return read


def diagonal_of(value):
    eye = lax.broadcasted_iota(jnp.int32, (TILE, TILE), 0) == lax.broadcasted_iota(jnp.int32, (TILE, TILE), 1)
    return jnp.sum(jnp.where(eye, value, 0.0), axis=0, keepdims=True) + epsilon


def flip_line(row):
    eye = lax.broadcasted_iota(jnp.int32, (TILE, TILE), 0) == lax.broadcasted_iota(jnp.int32, (TILE, TILE), 1)
    parts = [jnp.where(eye, row[:, i : i + TILE], 0.0) for i in range(0, row.shape[1], TILE)]
    return [jnp.sum(part, axis=1, keepdims=True) for part in parts]


def normalize_tiles(tiles, read, s_row, s_col, n_hi, n_lo):
    square = jnp.zeros((TILE, TILE), f32)
    for i, j in tiles:
        at, to = slice(i * TILE, (i + 1) * TILE), slice(j * TILE, (j + 1) * TILE)
        normed = read((i, j)) * s_col[i] * s_row[:, to]
        n_hi[at, to], n_lo[at, to] = halves(normed)
        if i == j:
            square = square + normed * normed
        else:
            square = square + 2.0 * (normed * normed)
            n_hi[to, at], n_lo[to, at] = halves(normed.T)
    return jnp.sum(square, axis=0, keepdims=True)


def early_kernel(tiles, n_parts, *refs):
    parts, (n_hi, n_lo, own, d_ref, square_ref, tile_ref) = refs[:n_parts], refs[n_parts:]
    width = n_hi.shape[0]
    read = tile_reader(tiles, parts, tile_ref)
    d_row = jnp.concatenate([diagonal_of(read((i, i))) for i in range(width // TILE)], axis=1)
    d_ref[...] = d_row
    s_row = lax.rsqrt(d_row)
    square_ref[...] = normalize_tiles(tiles, read, s_row, flip_line(s_row), n_hi, n_lo)
    for i in range(0, width, SPAN):
        band = slice(i, i + SPAN)
        own[band, :] = three(dot, (n_hi[band, :], n_lo[band, :]), (n_hi[...], n_lo[...]))


def early(tiles, parts, width):
    return pl.pallas_call(
        functools.partial(early_kernel, tiles, len(parts)),
        out_shape=[shape((width, width), bf16)] * 2 + [shape((width, width)), shape((1, width)), shape((1, TILE))],
        in_specs=[VMEM] * len(parts),
        out_specs=[VMEM] * 5,
        scratch_shapes=[pltpu.VMEM((TILE, TILE), f32)],
        compiler_params=params(16),
        cost_estimate=cost(100 * width**3, 8 * width**2),
        name="early",
    )(*parts)


def columns_band(columns, band):
    high = jnp.concatenate([hi[band, :] for hi, _ in columns], axis=1)
    low = jnp.concatenate([lo[band, :] for _, lo in columns], axis=1)
    return high, low


def ends(last):
    if not last:
        return 0, BLK
    swapped = lax.axis_index("pair") == 0
    return pl.multiple_of(jnp.where(swapped, BLK, 0), BLK), pl.multiple_of(jnp.where(swapped, 0, BLK), BLK)


def newton_kernel(tiles, n_parts, blocks, n_columns, last, *refs):
    refs = list(refs)

    def take(n):
        got = refs[:n]
        del refs[:n]
        return got

    parts = take(n_parts)
    known = [take(5) for _ in blocks]
    columns = [take(2) for _ in range(n_columns)]
    out_s, out_q = take(2)
    if last:
        tile_ref = take(1)[0]
    n_hi, n_lo, a_hi, a_lo, b_hi, b_lo = take(6)
    if not last:
        d_out, f_out, tile_ref = refs
    width = n_hi.shape[0]
    read = tile_reader(tiles, parts, tile_ref)

    d_parts = [block[3][...] for block in known]
    for i in range(blocks[-1][1] // TILE, width // TILE):
        d_parts.append(diagonal_of(read((i, i))))
    d_row = jnp.concatenate(d_parts, axis=1)
    s_row = lax.rsqrt(d_row)
    square = normalize_tiles(tiles, read, s_row, flip_line(s_row), n_hi, n_lo)
    for (lo, hi), block in zip(blocks, known):
        n_hi[lo:hi, lo:hi] = block[0][...]
        n_lo[lo:hi, lo:hi] = block[1][...]
        square = square + block[4][...]
    spread = jnp.full((1, 1), 1.5, f32) * jnp.sqrt(jnp.sum(square, axis=1, keepdims=True) / width)
    inverse = 1.0 / spread
    factor = 0.0625 * jnp.sqrt(d_row) * lax.rsqrt(spread)
    scale = 16.0 * s_row * factor
    s_col = flip_line(s_row)
    if not last:
        d_out[...] = d_row
        f_out[...] = factor

    for i in range(0, width, SPAN):
        band = slice(i, i + SPAN)
        inside = [k for k, (lo, hi) in enumerate(blocks) if lo <= i < hi]
        if inside:
            lo, hi = blocks[inside[0]]
            rest_ = slice(hi, width) if lo == 0 else slice(0, lo)
            own = three(dot, (n_hi[band, rest_], n_lo[band, rest_]), (n_hi[rest_, lo:hi], n_lo[rest_, lo:hi]))
            own = own + known[inside[0]][2][i - lo : i - lo + SPAN, :]
            other = three(dot, (n_hi[band, :], n_lo[band, :]), (n_hi[:, rest_], n_lo[:, rest_]))
            product = jnp.concatenate([own, other] if lo == 0 else [other, own], axis=1)
        else:
            product = three(dot, (n_hi[band, :], n_lo[band, :]), (n_hi[...], n_lo[...]))
        scaled = (n_hi[band, :].astype(f32) + n_lo[band, :].astype(f32)) * inverse
        product = product * (inverse * inverse)
        here = lax.broadcasted_iota(jnp.int32, (SPAN, width), 0) + i == lax.broadcasted_iota(jnp.int32, (SPAN, width), 1)
        weight = jnp.concatenate(s_col[i // TILE : (i + SPAN) // TILE], axis=0)
        a_hi[band, :], a_lo[band, :] = halves((product - 3.0 * scaled + jnp.where(here, 4.0, 0.0)) * weight)
        b_hi[band, :], b_lo[band, :] = halves(product - 6.0 * scaled + jnp.where(here, 5.0, 0.0))
    swapped = lax.axis_index("pair") == 0
    s_at, q_at = ends(last)
    for i in range(0, out_s.shape[0], BAND):
        band = slice(i, i + BAND)
        high, low = columns_band(columns, band)
        w = halves(three(dot, (high, low), (a_hi[...], a_lo[...])))
        plain = (high.astype(f32) + low.astype(f32)) * scale
        near_cols, far_cols = pl.ds(q_at, BLK), pl.ds(s_at, BLK)
        s_value = three(dot, w, (b_hi[:, far_cols], b_lo[:, far_cols]))
        q_value = three(dot, w, (b_hi[:, near_cols], b_lo[:, near_cols]))
        left, right, f_left, f_right = plain[:, :BLK], plain[:, BLK:], factor[:, :BLK], factor[:, BLK:]
        if last:
            left, right = jnp.where(swapped, right, left), jnp.where(swapped, left, right)
            f_left, f_right = jnp.where(swapped, f_right, f_left), jnp.where(swapped, f_left, f_right)
        out_s[band, :] = s_value * f_left + left
        out_q[band, :] = q_value * f_right + right


def newton(tiles, parts, blocks, known, columns, last):
    rows = columns[0][0].shape[0]
    width = sum(hi.shape[1] for hi, _ in columns)
    flat = list(parts) + [v for block in known for v in block] + [h for both in columns for h in both]
    outs = [shape((rows, BLK))] * 2
    scratch = [pltpu.VMEM((TILE, TILE), f32)]
    if last:
        scratch += [pltpu.VMEM((width, width), bf16)] * 6
    else:
        outs += [shape((width, width), bf16)] * 6 + [shape((1, width))] * 2
    return pl.pallas_call(
        functools.partial(newton_kernel, tiles, len(parts), blocks, len(columns), last),
        out_shape=outs,
        in_specs=[VMEM] * len(flat),
        out_specs=[VMEM] * len(outs),
        scratch_shapes=scratch,
        compiler_params=params(28),
        cost_estimate=cost(3 * (width**3 + 2 * rows * width**2), 16 * width**2),
        name="newton",
    )(*flat)


def power_kernel(n_hi, n_lo, a_hi, a_lo, b_hi, b_lo, d_ref, p_hi, p_lo, t_hi, t_lo):
    width = n_hi.shape[0]
    d_col = flip_line(d_ref[...])
    for i in range(0, width, BAND):
        band = slice(i, i + BAND)
        here = lax.broadcasted_iota(jnp.int32, (BAND, width), 0) + i == lax.broadcasted_iota(jnp.int32, (BAND, width), 1)
        root = jnp.sqrt(jnp.concatenate(d_col[i // TILE : (i + BAND) // TILE], axis=0))
        value = three(dot, (a_hi[band, :], a_lo[band, :]), (b_hi[...], b_lo[...]))
        p_hi[band, :], p_lo[band, :] = halves(value * (0.125 * root) + jnp.where(here, 2.0, 0.0))
    for i in range(0, width, BAND):
        band = slice(i, i + BAND)
        value = three(dot, (n_hi[band, :], n_lo[band, :]), (p_hi[...], p_lo[...]))
        t_hi[band, :], t_lo[band, :] = halves(value)


def powers(n_hi, n_lo, a_hi, a_lo, b_hi, b_lo, d_row):
    width = n_hi.shape[0]
    return pl.pallas_call(
        power_kernel,
        out_shape=[shape((width, width), bf16)] * 4,
        in_specs=[VMEM] * 7,
        out_specs=[VMEM] * 4,
        compiler_params=params(24),
        cost_estimate=cost(3 * 2 * width**3, 16 * width**2),
        name="powers",
    )(n_hi, n_lo, a_hi, a_lo, b_hi, b_lo, d_row)


def next_kernel(p_hi, p_lo, t_hi, t_lo, f_ref, s_out, q_out):
    f_row = f_ref[...] * 8.0
    f_col = flip_line(f_row)
    for out, base in ((s_out, 0), (q_out, BLK)):
        place = {t: k for k, t in enumerate(triangle(0, BLK // TILE))}
        for i in range(base, base + BLK, SPAN):
            cols = slice(base, i + SPAN)
            full = three(dot, (p_hi[i : i + SPAN, :], p_lo[i : i + SPAN, :]), (t_hi[:, cols], t_lo[:, cols]))
            for at in range(i, i + SPAN, TILE):
                for j in range(base, at + TILE, TILE):
                    tile = full[at - i : at - i + TILE, j - base : j - base + TILE]
                    tile = tile * f_col[at // TILE] * f_row[:, j : j + TILE]
                    out[place[((at - base) // TILE, (j - base) // TILE)]] = tile


def next_grams(p_hi, p_lo, t_hi, t_lo, f_row):
    width = p_hi.shape[0]
    n = len(triangle(0, BLK // TILE))
    return pl.pallas_call(
        next_kernel,
        out_shape=[shape((n, TILE, TILE))] * 2,
        in_specs=[VMEM] * 5,
        out_specs=[VMEM] * 2,
        compiler_params=params(16),
        cost_estimate=cost(3 * 0.5 * width**3, 8 * width**2),
        name="next_grams",
    )(p_hi, p_lo, t_hi, t_lo, f_row)


def cross_kernel(groups, near, far, near_hi, near_lo, far_hi, far_lo, *rest):
    outs, packed = rest[:-1], rest[-1]
    near_hi[...], near_lo[...] = halves(near[...])
    far_hi[...], far_lo[...] = halves(far[...])
    count = BLK // TILE
    for i in range(0, BLK, SPAN):
        left = (far_hi[:, i : i + SPAN], far_lo[:, i : i + SPAN])
        full = three(dot_t, left, (near_hi[...], near_lo[...]))
        for a in range(0, SPAN, TILE):
            for b in range(0, BLK, TILE):
                packed[(i + a) // TILE * count + b // TILE] = full[a : a + TILE, b : b + TILE]
    spread_tiles(packed, None, outs, groups)


def cross_tiles():
    count = BLK // TILE
    return [(count + i, j) for i in range(count) for j in range(count)]


def cross(near, far):
    rows = near.shape[0]
    tiles = cross_tiles()
    n = len(tiles)
    groups = lax.axis_size("rows")
    outs = [shape((rows, BLK), bf16)] * 4 + part_shapes(tiles, groups)
    out = pl.pallas_call(
        functools.partial(cross_kernel, groups),
        out_shape=outs,
        in_specs=[VMEM] * 2,
        out_specs=[VMEM] * len(outs),
        scratch_shapes=[pltpu.VMEM((n, TILE, TILE), f32)],
        compiler_params=params(16),
        cost_estimate=cost(3 * rows * BLK * BLK, 16 * rows * BLK),
        name="cross",
    )(near, far)
    return (out[0], out[1]), (out[2], out[3]), out[4:]


def around(x, pairs, hop):
    return lax.ppermute(x, "pair", [(i, (i + 2 * hop) % pairs) for i in range(pairs)])


def after(values, first):
    return lax.optimization_barrier((values, first))[0]


def place_kernel(near, start, block, kept, out, sem):
    core = lax.rem(lax.axis_index("pair"), 2)
    at = 1 - core if near else core
    cols = pl.ds(pl.multiple_of(at * BLK, BLK), BLK)
    copy = pltpu.make_async_copy(block, out.at[start : start + block.shape[0], cols], sem)
    copy.start()
    copy.wait()


def place(block, start, out, rows):
    first = out is None
    call = pl.pallas_call(
        functools.partial(place_kernel, first, start),
        out_shape=shape((rows, 2 * BLK)),
        in_specs=[VMEM, SMEM if first else ANY],
        out_specs=ANY,
        scratch_shapes=[pltpu.SemaphoreType.DMA],
        input_output_aliases={} if first else {1: 0},
        compiler_params=params(16),
        name="place",
    )
    return call(block, jnp.zeros((1,), f32) if first else out)


def per_device(matrix, plan):
    pairs = lax.axis_size("pair")
    hops = pairs // 2
    near, own_q, own_s = pick(matrix, plan, pairs)
    near = swap_near(near, pairs)
    s_mine = [own_s[0]] + [around(own_s[k], pairs, k) for k in range(1, hops)]
    forward, *queues = merge(near, own_q)
    s_theirs = [forward[0]] + [around(forward[k], pairs, k) for k in range(1, hops)]
    arrived = [s_mine + s_theirs]
    gate = [s_mine, s_theirs[1]]
    columns, groups = [], []
    done, spread = [], []
    for index, chunks in enumerate(ROUNDS):
        for chunk in chunks:
            if chunk:
                queue = after(queues[chunk - 1], gate)
                arrived.append([queue[0]] + [around(queue[k], pairs, k) for k in range(1, hops)])
        both, parts = gram([arrived[chunk] for chunk in chunks], columns, index, pairs)
        columns += both
        gate = parts
        got = sum_first(parts)
        done = after(sum_second(parts, got, done), spread)
        spread = sum_spread(done)
        groups.append(spread)
    edge = sum(CHUNKS[k][2] for k in ROUNDS[0])
    known = early(round_tiles(0), groups[0], edge)
    out_s, out_q, *squares, d_row, f_row = newton(round_tiles(1), groups[1], [(0, edge)], [known], columns, False)
    far, near = swap_far(out_s, pairs), swap_near(out_q, pairs)
    power = powers(*squares, d_row)
    near, far = after((near, far), power)
    near_pair, far_pair, parts = cross(near, far)
    s_gram, q_gram = next_grams(*after(power, parts), f_row)
    far_gram = swap_far(s_gram, pairs)
    near_gram = swap_near(q_gram, pairs)
    summed = sum_rows(parts)
    count = BLK // TILE
    known = [early(triangle(0, count), [tiles], BLK) for tiles in (near_gram, far_gram)]
    crossing = cross_tiles()
    columns = [near_pair, far_pair]
    out_s, out_q = newton(crossing, summed, [(0, BLK), (BLK, 2 * BLK)], known, columns, True)
    far, near = swap_far(out_s, pairs), swap_near(out_q, pairs)
    return place(far, 0, place(near, 0, None, near.shape[0]), near.shape[0])


def solution(mesh):
    placed = (P(("rows", "pair"), None), P())
    return jax.shard_map(
        per_device, mesh=mesh, in_specs=placed, out_specs=P("rows", "pair"), check_vma=False
    )
```
